128 devices in a mesh: sib: 2 (over z_lo), row: 8 (over z_hi, y), col: 8 (over x, core).
Axes of the slice: x: 4, y: 4, z: 4 (z_hi: 2, z_lo: 2; z = z_hi * 2 + z_lo), core: 2. Of those that a mesh axis runs over, the one named last changes fastest.
Arguments:
- child_upd: float32 [2, 8192, 8192], P('sib', 'row', 'col'), may hold values from -6 to 6
- child_map: int32 [2, 64], replicated, may hold values from 0 to 159, as said below
- orig_pivot: float32 [512, 512], replicated, may hold values from -6 to 200, as said below
Outputs:
- factored_front: float32 [20480, 20480], P('row', ('sib', 'col'))
The draws below stay inside these ranges and needn't reach their ends.
Inputs may be any that keep to these rules, and one draw needn't show every extreme that they name: For each child c the entries child_map[c, :] are distinct. Child front block g lies on child grid row and column (g // 2) % 8; parent block b lies on parent grid row (b // 2) % 8 and column group (b // 2) % 16. Of one child's blocks on one child grid row, exactly 1 map to each parent grid row; of one child's blocks that map to one parent grid row, exactly half have (b // 2) // 8 even. `orig_pivot`: the diagonal lies between 100 and 200.
All inputs are finite; a program needn't handle non-finite values.
Results may differ from the reference program's by a relative error of at most 0.0001.
Values sent between devices are 32-bit elements; how exact they have to be, the bound alone decides.
No kernel may reach another device: no remote copies, remote signals or barrier semaphores. Data moves between devices by JAX's collectives and lax.ppermute only.
A program may use at most 192 MiB of HBM per device.

```python
import jax
import jax.numpy as jnp
from jax import lax

BLK = 128
TILE = 256
NF = 20480
NC = 8192
PANELS = 2
FS = 512
N_SIB = 2
N_ROW = 8
N_COL = 8


def build_map(key, child_index):
    child_key = jax.random.fold_in(key, child_index)
    key_class, key_half, key_slot = jax.random.split(child_key, 3)
    per_dev = NC // (BLK * N_ROW)
    per_class = per_dev // N_ROW
    halfway = per_dev // 2
    slot_count = NF // (2 * BLK * N_ROW)
    class_perm = jax.vmap(lambda one_key: jax.random.permutation(one_key, per_dev))(jax.random.split(key_class, N_ROW))
    classes = (class_perm % N_ROW).astype(jnp.int32)
    places = jnp.arange(per_dev, dtype=jnp.int32)
    same = (classes[:, :, None] == classes[:, None, :]) & (places[None, None, :] < places[None, :, None])
    rank_in = jnp.sum(same.astype(jnp.int32), axis=2)
    sources = jnp.arange(N_ROW, dtype=jnp.int32)[:, None]
    position = sources * per_class + rank_in
    shuffle = jax.vmap(lambda one_key: jax.random.permutation(one_key, per_dev))(jax.random.split(key_half, N_ROW)).astype(jnp.int32)
    drawn = shuffle[classes, position]
    halves = (drawn >= halfway).astype(jnp.int32)
    ranks = drawn % halfway
    scores = jax.random.randint(key_slot, (N_ROW, 2, slot_count), 0, 1 << 20) * slot_count + jnp.arange(slot_count, dtype=jnp.int32)
    if child_index == 0:
        grid_d = jnp.arange(N_ROW)[:, None, None]
        grid_h = jnp.arange(2)[None, :, None]
        grid_q = jnp.arange(slot_count)[None, None, :]
        forced = (grid_d == 0) & (grid_h == 0) & (grid_q == 0) | (grid_d == N_ROW - 1) & (grid_h == 1) & (grid_q == slot_count - 1)
        scores = jnp.where(forced, -1, scores)
    slot_order = jnp.argsort(scores, axis=-1).astype(jnp.int32)
    slots = slot_order[classes, halves, ranks]
    parent_tile = (2 * (slots // 2) + halves) * N_ROW + classes
    parent_block = (2 * parent_tile + slots % 2).astype(jnp.int32)
    global_block = 2 * (places[None, :] // 2 * N_ROW + sources) + places[None, :] % 2
    return jnp.zeros((NC // BLK,), jnp.int32).at[global_block.reshape(-1)].set(parent_block.reshape(-1))


def draw_child_map(key, part):
    key = jax.random.fold_in(key, 11)
    return jnp.stack([build_map(key, 0), build_map(key, 1)])


def draw_orig_pivot(key, part):
    key = jax.random.fold_in(key, 23)
    key_off, key_diag = jax.random.split(key)
    off_diag = jnp.clip(jax.random.normal(key_off, (FS, FS), jnp.float32), -6.0, 6.0)
    diagonal = jax.random.uniform(key_diag, (FS,), jnp.float32, 100.0, 200.0)
    on_diag = jnp.arange(FS)[:, None] == jnp.arange(FS)[None, :]
    return jnp.where(on_diag, diagonal[:, None], off_diag)


def steps_of(stream_key, shape, cuts, low, top_value):
    factor_of, own = 1.0, jax.random.fold_in(stream_key, 6)
    for dim, shards_of in cuts:
        steps = jnp.exp(jax.random.uniform(jax.random.fold_in(own, dim), (shards_of,), jnp.float32, low / len(cuts), top_value / len(cuts)))
        factor_of = factor_of * jnp.repeat(steps, shape[dim] // shards_of).reshape([-1 if axis == dim else 1 for axis in range(len(shape))])
    return factor_of


def bell_draw(stream_key, dims, width, bound, pieces=(), kind=jnp.bfloat16):
    loudness = steps_of(stream_key, dims, pieces, -0.22, 0.18) if pieces else 1.0
    result = jax.random.normal(stream_key, dims, jnp.float32) * width * loudness
    return jnp.minimum(jnp.maximum(result, -bound), bound).astype(kind)


def setup_inputs(seed: int = 0) -> dict:
    key_list = jax.random.split(jax.random.key(seed), 4)
    return {
        "child_upd": bell_draw(key_list[0], (2, NC, NC), 1.0, 6.0, ((0, 2), (1, 8), (2, 8)), jnp.float32),
        "child_map": draw_child_map(jax.random.fold_in(key_list[3], 71), 0),
        "orig_pivot": draw_orig_pivot(jax.random.fold_in(key_list[3], 71), 0),
    }


def product(left, right):
    return jnp.dot(left, right, precision=lax.Precision.HIGHEST, preferred_element_type=jnp.float32)


def factor(square):
    extent = square.shape[0]
    if extent == 1:
        unit_one = jnp.ones((1, 1), jnp.float32)
        return unit_one, square, unit_one, 1.0 / square
    middle = extent // 2
    top_lower, top_upper, top_linv, top_uinv = factor(square[:middle, :middle])
    right_part = product(top_linv, square[:middle, middle:])
    left_part = product(square[middle:, :middle], top_uinv)
    low_lower, low_upper, low_linv, low_uinv = factor(square[middle:, middle:] - product(left_part, right_part))
    zero_block = jnp.zeros((middle, extent - middle), jnp.float32)
    lower_unit = jnp.concatenate([jnp.concatenate([top_lower, zero_block], 1), jnp.concatenate([left_part, low_lower], 1)], 0)
    upper_part = jnp.concatenate([jnp.concatenate([top_upper, right_part], 1), jnp.concatenate([zero_block.T, low_upper], 1)], 0)
    lower_inv = jnp.concatenate([jnp.concatenate([top_linv, zero_block], 1), jnp.concatenate([-product(low_linv, product(left_part, top_linv)), low_linv], 1)], 0)
    upper_inv = jnp.concatenate([jnp.concatenate([top_uinv, -product(product(top_uinv, right_part), low_uinv)], 1), jnp.concatenate([zero_block.T, low_uinv], 1)], 0)
    return lower_unit, upper_part, lower_inv, upper_inv


def reference(child_upd, child_map, orig_pivot):
    row_count = N_ROW
    group_count = N_SIB * N_COL
    per_dev = NC // (BLK * N_ROW)
    front_rows = NF // row_count
    front_cols = NF // group_count
    col_slots = front_cols // BLK
    sources = jnp.arange(row_count, dtype=jnp.int32)[:, None]
    places = jnp.arange(per_dev, dtype=jnp.int32)[None, :]
    global_block = (2 * ((places // 2) * row_count + sources) + places % 2).astype(jnp.int32)
    offsets = jnp.arange(BLK, dtype=jnp.int32)
    front_part = jnp.zeros((NF, NF), jnp.float32)
    for child_index in range(2):
        target = child_map[child_index][global_block]
        parent_tiles = target // 2
        classes = parent_tiles % row_count
        halves = (parent_tiles // row_count) % 2
        row_block = classes * (front_rows // BLK) + 2 * (parent_tiles // row_count) + target % 2
        col_block = (halves * row_count + classes) * col_slots + 2 * (parent_tiles // group_count) + target % 2
        row_index = (row_block.reshape(-1)[:, None] * BLK + offsets[None, :]).reshape(NC)
        col_index = (col_block.reshape(-1)[:, None] * BLK + offsets[None, :]).reshape(NC)
        spread = jnp.zeros((NF, NC), jnp.float32).at[row_index].add(child_upd[child_index])
        front_part = front_part.at[:, col_index].add(spread)
    for tile_row in range(PANELS):
        for tile_col in range(PANELS):
            row_start = (tile_row % row_count) * front_rows + (tile_row // row_count) * TILE
            col_start = (tile_col % group_count) * front_cols + (tile_col // group_count) * TILE
            piece = orig_pivot[tile_row * TILE:(tile_row + 1) * TILE, tile_col * TILE:(tile_col + 1) * TILE]
            front_part = front_part.at[row_start:row_start + TILE, col_start:col_start + TILE].add(piece)
    storage = jnp.arange(NF, dtype=jnp.int32)
    row_tile = ((storage % front_rows) // TILE) * row_count + storage // front_rows
    col_tile = ((storage % front_cols) // TILE) * group_count + storage // front_cols
    identity_tile = jnp.eye(TILE, dtype=jnp.float32)
    for panel_index in range(PANELS):
        row_start = (panel_index % row_count) * front_rows + (panel_index // row_count) * TILE
        col_start = (panel_index % group_count) * front_cols + (panel_index // group_count) * TILE
        pivot_tile = front_part[row_start:row_start + TILE, col_start:col_start + TILE]
        lower_unit, upper_part, lower_inv, upper_inv = factor(pivot_tile)
        below_mask = (row_tile > panel_index)[:, None]
        right_mask = (col_tile > panel_index)[None, :]
        column = front_part[:, col_start:col_start + TILE]
        multipliers = jnp.where(below_mask, product(column, upper_inv), 0.0)
        upper_rows = jnp.where(right_mask, product(lower_inv, front_part[row_start:row_start + TILE, :]), 0.0)
        front_part = front_part - product(multipliers, upper_rows)
        front_part = front_part.at[:, col_start:col_start + TILE].set(jnp.where(below_mask, multipliers, front_part[:, col_start:col_start + TILE]))
        front_part = front_part.at[row_start:row_start + TILE, :].set(jnp.where(right_mask, upper_rows, front_part[row_start:row_start + TILE, :]))
        packed = lower_unit - identity_tile + upper_part
        front_part = front_part.at[row_start:row_start + TILE, col_start:col_start + TILE].set(packed)
    return front_part
```

```python
import jax
import jax.numpy as jnp
from jax import lax
from jax.experimental import pallas as pl
from jax.experimental.pallas import tpu as pltpu
from jax.sharding import PartitionSpec as P

BLK = 128
TILE = 256
NF = 20480
PANELS = 2
FS = PANELS * TILE
NROW = 8
NCOL = 8
PER = 8
FRONT_ROWS = NF // NROW
FRONT_COLS = NF // (2 * NCOL)
ROW_SLOTS = FRONT_ROWS // BLK
MSG = BLK + 32 + 8
F32 = jnp.float32
VMEM = pl.BlockSpec(memory_space=pltpu.VMEM)
SMEM = pl.BlockSpec(memory_space=pltpu.SMEM)
LIMIT = 56 * 2**20


def product(left, right):
    return jnp.dot(left, right, precision=lax.Precision.HIGHEST, preferred_element_type=F32)


def split(value):
    high = value.astype(jnp.bfloat16)
    low = (value - high.astype(F32)).astype(jnp.bfloat16)
    return high, low


def product3(left, right):
    dot = lambda a, b: jnp.dot(a, b, preferred_element_type=F32)
    return dot(left[0], right[0]) + (dot(left[0], right[1]) + dot(left[1], right[0]))


def target(maps, child, line, place):
    return maps[child, 2 * ((place // 2) * NROW + line) + place % 2]


def class_of(block):
    return (block // 2) % NROW


def half_of(block):
    return (block // 2) // NROW % 2


def row_slot(block):
    return 2 * (block // 2 // NROW) + block % 2


def col_slot(block):
    return 2 * (block // 2 // (2 * NCOL)) + block % 2


def place_of(maps, child, line, wanted):
    found = jnp.int32(0)
    block = jnp.int32(0)
    for place in range(PER):
        here = target(maps, child, line, place)
        hit = class_of(here) == wanted
        found = jnp.where(hit, place, found)
        block = jnp.where(hit, here, block)
    return found, block


def at(index, size):
    return pl.ds(pl.multiple_of(index * size, size), size)


def pack_cols_kernel(maps, ids, x_ref, pivot_ref, *out_refs):
    child, row, col = ids[0], ids[1], ids[2]
    pivot_ref[...] = jnp.zeros_like(pivot_ref)
    ends = [place_of(maps, child, col, wanted) for wanted in range(PANELS)]
    for a in range(PANELS):
        p, t = place_of(maps, child, row, a)
        for b in range(PANELS):
            q, u = ends[b]

            @pl.when((t // 2 == a) & (u // 2 == b))
            def _():
                pivot_ref[at(t, BLK), at(u, BLK)] = x_ref[at(p, BLK), at(q, BLK)]

    for d in range(NCOL):
        dest = col ^ d
        q, _ = place_of(maps, child, col, dest)
        out = out_refs[d]
        out[: PER * BLK, :] = x_ref[:, at(q, BLK)]
        for b in range(PANELS):
            for p in range(PER):
                start = PER * BLK + b * BLK + p * 16
                out[start : start + 16, :] = x_ref[
                    pl.ds(pl.multiple_of(p * BLK + dest * 16, 16), 16), at(ends[b][0], BLK)
                ]


def pack_cols(maps, ids, x):
    message = jax.ShapeDtypeStruct(((PER + PANELS) * BLK, BLK), F32)
    return pl.pallas_call(
        pack_cols_kernel,
        out_shape=[jax.ShapeDtypeStruct((FS, FS), F32)] + [message] * NCOL,
        in_specs=[SMEM, SMEM, VMEM],
        out_specs=[VMEM] * (NCOL + 1),
        compiler_params=pltpu.CompilerParams(vmem_limit_bytes=LIMIT),
        cost_estimate=pl.CostEstimate(flops=0, bytes_accessed=10 * 2**20, transcendentals=0),
    )(maps, ids, x)


def pack_rows_kernel(maps, ids, *refs):
    in_refs, out, thin = refs[:NCOL], refs[NCOL], refs[NCOL + 1]
    child, row, col = ids[0], ids[1], ids[2]
    thin[...] = jnp.zeros_like(thin)
    places = [place_of(maps, child, row, wanted)[0] for wanted in range(NROW)]
    blocks = [place_of(maps, child, j, col)[1] for j in range(NCOL)]
    for d in range(NCOL):
        source = col ^ d
        _, u = place_of(maps, child, source, col)
        half = half_of(u)
        rank = jnp.int32(0)
        for j in range(NCOL):
            rank += jnp.where((j < source) & (half_of(blocks[j]) == half), 1, 0)
        lanes = at(rank, BLK)
        for dest in range(NROW):
            out[half * NROW + dest, :BLK, lanes] = in_refs[d][at(places[dest], BLK), :]
            for a in range(PANELS):
                out[half * NROW + dest, BLK + 16 * a : BLK + 16 * (a + 1), lanes] = in_refs[d][
                    pl.ds(pl.multiple_of(places[a] * BLK + dest * 16, 16), 16), :
                ]
        for b in range(PANELS):
            _, v = place_of(maps, child, source, b)

            @pl.when(v // 2 == b)
            def _():
                start = PER * BLK + b * BLK
                thin[:, at(v, BLK)] = in_refs[d][start : start + BLK, :]

    for half in range(2):
        for dest in range(NROW):
            out[half * NROW + dest, BLK + 32 :, :] = thin[
                pl.ds(pl.multiple_of(places[dest] * 16 + half * 8, 8), 8), :
            ]


def pack_rows(maps, ids, pieces):
    return pl.pallas_call(
        pack_rows_kernel,
        out_shape=jax.ShapeDtypeStruct((2 * NROW, MSG, FS), F32),
        in_specs=[SMEM, SMEM] + [VMEM] * NCOL,
        out_specs=VMEM,
        scratch_shapes=[pltpu.VMEM((BLK, FS), F32)],
        compiler_params=pltpu.CompilerParams(vmem_limit_bytes=LIMIT),
        cost_estimate=pl.CostEstimate(flops=0, bytes_accessed=10 * 2**20, transcendentals=0),
    )(maps, ids, *pieces)


def thin_rows_kernel(maps, ids, in_ref, rows_ref, cols_ref):
    rows_ref[...] = jnp.zeros_like(rows_ref)
    for source in range(2 * NROW):
        child, line = source // NROW, source % NROW
        cols_ref[source * 8 : (source + 1) * 8, :] = in_ref[source, BLK + 32 :, :]
        for a in range(PANELS):
            _, t = place_of(maps, child, line, a)

            @pl.when(t // 2 == a)
            def _():
                rows_ref[pl.ds(pl.multiple_of(child * 64 + t * 16, 16), 16), :] = in_ref[
                    source, BLK + 16 * a : BLK + 16 * (a + 1), :
                ]


def thin_rows(maps, ids, arrived):
    out = jax.ShapeDtypeStruct((BLK, FS), F32)
    return pl.pallas_call(
        thin_rows_kernel,
        out_shape=(out, out),
        in_specs=[SMEM, SMEM, VMEM],
        out_specs=(VMEM, VMEM),
        compiler_params=pltpu.CompilerParams(vmem_limit_bytes=LIMIT),
        cost_estimate=pl.CostEstimate(flops=0, bytes_accessed=2 * 2**20, transcendentals=0),
    )(maps, ids, arrived)


def column_slots(maps, ids):
    sib, col = ids[0], ids[2]
    slots = []
    for child in range(2):
        count = jnp.int32(0)
        found = [jnp.int32(0)] * 4
        for j in range(NCOL):
            _, u = place_of(maps, child, j, col)
            mine = half_of(u) == sib
            for r in range(4):
                found[r] = jnp.where(mine & (count == r), col_slot(u), found[r])
            count += jnp.where(mine, 1, 0)
        slots.append(found)
    return slots


def assemble_kernel(maps, ids, in_ref, out_ref):
    row = ids[1]
    out_ref[...] = jnp.zeros_like(out_ref)
    slots = column_slots(maps, ids)
    for source in range(2 * NROW):
        child, line = source // NROW, source % NROW
        _, t = place_of(maps, child, line, row)
        rows = at(row_slot(t), BLK)
        for r in range(4):
            out_ref[rows, at(slots[child][r], BLK)] += in_ref[source, :BLK, r * BLK : (r + 1) * BLK]


def assemble(maps, ids, arrived):
    return pl.pallas_call(
        assemble_kernel,
        out_shape=jax.ShapeDtypeStruct((FRONT_ROWS, FRONT_COLS), F32),
        in_specs=[SMEM, SMEM, VMEM],
        out_specs=VMEM,
        compiler_params=pltpu.CompilerParams(vmem_limit_bytes=LIMIT),
        cost_estimate=pl.CostEstimate(flops=0, bytes_accessed=20 * 2**20, transcendentals=0),
    )(maps, ids, arrived)


def invert_block(a, state, rows):
    n = BLK
    lane8 = lax.broadcasted_iota(jnp.int32, (8, n), 1)
    row8 = lax.broadcasted_iota(jnp.int32, (8, n), 0)
    row = lax.broadcasted_iota(jnp.int32, (n, n), 0)
    lane = lax.broadcasted_iota(jnp.int32, (n, n), 1)

    def group(g, carry):
        s, cols = carry
        state[...] = s
        t8 = state[at(g, 8), :]
        saved = []
        for t in range(8):
            c8 = jnp.broadcast_to(t8[:, t : t + 1], (8, n))
            pivot_row = t8[t : t + 1, :]
            inv8 = 1.0 / jnp.broadcast_to(c8[t : t + 1, :], (8, n))
            saved.append(pivot_row)
            r8 = jnp.where(lane8 == t, 1.0, jnp.broadcast_to(pivot_row, (8, n))) * inv8
            t8 = jnp.where(row8 == t, r8, jnp.where(lane8 == t, 0.0, t8) - c8 * r8)
            r = jnp.broadcast_to(r8[0:1, :], (n, n))
            inv = jnp.broadcast_to(inv8[0:1, :], (n, n))
            c = jnp.broadcast_to(s[:, t : t + 1], (n, n))
            cols = jnp.where(lane == t, c * inv, cols)
            s = jnp.where(row == g * 8 + t, r, jnp.where(lane == t, 0.0, s) - c * r)
        rows[at(g, 8), :] = pltpu.roll(jnp.concatenate(saved, 0), g * 8, 1)
        return pltpu.roll(s, n - 8, 1), pltpu.roll(cols, n - 8, 1)

    inverse, cols = lax.fori_loop(0, n // 8, group, (a, jnp.zeros((n, n), F32)))
    saved = rows[...]
    eye = row == lane
    packed = jnp.where(row > lane, cols, saved)
    lower_inv = jnp.where(row > lane, saved, jnp.where(eye, 1.0, 0.0))
    upper_inv = jnp.where(row < lane, -cols, jnp.where(eye, 1.0 / saved, 0.0))
    return inverse, packed, lower_inv, upper_inv


def factor_kernel(ids, pieces_ref, orig_ref, inv_ref, linv_ref, uinv_ref, lu_ref, state, rows):
    count, n = FS // BLK, BLK
    row, col = ids[1], ids[2]
    inv_ref[...] = orig_ref[...]
    for q in range(NROW * NCOL):
        dy = 4 * (q & 1) + (q & 2) + (q >> 2 & 1)
        dx = 4 * (q >> 3 & 1) + (q >> 3 & 2) + (q >> 5 & 1)
        place = at((row ^ dy) * NCOL + (col ^ dx), 8)
        inv_ref[place, :] += pieces_ref[q * 8 : (q + 1) * 8, :]
    linv_ref[...] = jnp.zeros_like(linv_ref)
    uinv_ref[...] = jnp.zeros_like(uinv_ref)
    for k in range(count):
        lo, hi = k * n, (k + 1) * n
        inverse, packed, lower_inv, upper_inv = invert_block(inv_ref[lo:hi, lo:hi], state, rows)
        x = inv_ref[lo:hi, :]
        y = inv_ref[:, lo:hi]
        scaled_rows = product(lower_inv, x)
        scaled_cols = product(y, upper_inv)
        lu_ref[lo:hi, lo:hi] = packed
        linv_ref[lo:hi, lo:hi] = lower_inv
        uinv_ref[lo:hi, lo:hi] = upper_inv
        if k > 0:
            linv_ref[lo:hi, :lo] = scaled_rows[:, :lo]
            uinv_ref[:lo, lo:hi] = -scaled_cols[:lo]
        if k < count - 1:
            lu_ref[lo:hi, hi:] = scaled_rows[:, hi:]
            lu_ref[hi:, lo:hi] = scaled_cols[hi:]
        inv_ref[lo:hi, :] = product(inverse, x)
        inv_ref[lo:hi, lo:hi] = inverse
        x = inv_ref[lo:hi, :]
        for i in range(count):
            if i != k:
                a, b = i * n, (i + 1) * n
                inv_ref[a:b, lo:hi] = jnp.zeros((n, n), F32)
                inv_ref[a:b, :] = inv_ref[a:b, :] - product(y[a:b], x)


def factor(ids, pieces, orig):
    square = jax.ShapeDtypeStruct((FS, FS), F32)
    return pl.pallas_call(
        factor_kernel,
        out_shape=(square,) * 4,
        in_specs=[SMEM, VMEM, VMEM],
        out_specs=(VMEM,) * 4,
        scratch_shapes=[pltpu.VMEM((BLK, BLK), F32)] * 2,
        compiler_params=pltpu.CompilerParams(vmem_limit_bytes=LIMIT),
        cost_estimate=pl.CostEstimate(flops=30 * 10**9, bytes_accessed=6 * 2**20, transcendentals=0),
    )(ids, pieces, orig)


def update_kernel(
    maps, ids, front_ref, cols_ref, inv_ref, linv_ref, uinv_ref, lu_ref, *refs
):
    row_refs, out_ref = refs[:NROW], refs[NROW]
    dense, z_high, z_low, pivots = refs[NROW + 1 :]
    step = pl.program_id(0)
    sib, row, col = ids[0], ids[1], ids[2]
    group = sib * NCOL + col

    @pl.when(step == 0)
    def _():
        pivots[...] = jnp.zeros_like(pivots)
        slots = column_slots(maps, ids)
        for d in range(NROW):
            line = row ^ d
            for child in range(2):
                for b in range(4):
                    start = child * 64 + b * 16
                    rows = pl.ds(pl.multiple_of(b * BLK + line * 16, 16), 16)
                    for r in range(4):
                        pivots[rows, at(slots[child][r], BLK)] += row_refs[d][
                            start : start + 16, r * BLK : (r + 1) * BLK
                        ]
        right = pivots[...]
        z = product(inv_ref[...], right)
        high, low = split(z)
        z_high[...] = high
        z_low[...] = low

        dense[...] = jnp.zeros_like(dense)
        for child in range(2):
            for line in range(NROW):
                _, t = place_of(maps, child, line, row)
                source = (child * NROW + line) * 8
                start = row_slot(t) * BLK

                @pl.loop(0, 2 * NCOL)
                def _(owner):
                    rows = start + (owner % NCOL) * 16 + owner // NCOL * 8
                    dense[pl.ds(pl.multiple_of(rows, 8), 8), :] += cols_ref[
                        pl.ds(pl.multiple_of(owner * BLK + source, 8), 8), :
                    ]

    left = dense[at(step, TILE), :]
    out_ref[...] = front_ref[...] - product3(split(left), (z_high[...], z_low[...]))

    @pl.when(group < PANELS)
    def _():
        out_ref[:, :TILE] = product(left, uinv_ref[:, at(group, TILE)])

    @pl.when((step == 0) & (row < PANELS))
    def _():
        out_ref[...] = product(linv_ref[at(row, TILE), :], pivots[...])

        @pl.when(group < PANELS)
        def _():
            out_ref[:, :TILE] = lu_ref[at(row, TILE), at(group, TILE)]


def update(maps, ids, front, cols, factors, row_pieces):
    block = pl.BlockSpec((TILE, FRONT_COLS), lambda i: (i, 0))
    return pl.pallas_call(
        update_kernel,
        grid=(FRONT_ROWS // TILE,),
        out_shape=jax.ShapeDtypeStruct((FRONT_ROWS, FRONT_COLS), F32),
        in_specs=[SMEM, SMEM, block, VMEM] + [VMEM] * 4 + [VMEM] * NROW,
        out_specs=block,
        scratch_shapes=[
            pltpu.VMEM((FRONT_ROWS, FS), F32),
            pltpu.VMEM((FS, FRONT_COLS), jnp.bfloat16),
            pltpu.VMEM((FS, FRONT_COLS), jnp.bfloat16),
            pltpu.VMEM((FS, FRONT_COLS), F32),
        ],
        compiler_params=pltpu.CompilerParams(vmem_limit_bytes=LIMIT),
        cost_estimate=pl.CostEstimate(
            flops=6 * FRONT_ROWS * FRONT_COLS * FS, bytes_accessed=30 * 2**20, transcendentals=0
        ),
    )(maps, ids, front, cols, *factors, *row_pieces)


def swap(value, axis, size, distance):
    if distance == 0:
        return value
    return lax.ppermute(value, axis, [(i, i ^ distance) for i in range(size)])


def body(child_upd, child_map, orig_pivot):
    ids = jnp.stack([lax.axis_index("sib"), lax.axis_index("row"), lax.axis_index("col")])
    ids = ids.astype(jnp.int32)
    grid = ("row", "col")
    pivot, *messages = pack_cols(child_map, ids, child_upd[0])
    messages = [swap(m, "col", NCOL, d) for d, m in enumerate(messages)]
    parts = lax.all_to_all(
        pivot.reshape(NROW * NCOL, FS // (NROW * NCOL), FS), grid, 0, 0, tiled=True
    )
    part = jnp.sum(parts, axis=0)
    part = part + swap(part, "sib", 2, 1)
    for axis, distance in (("row", 4), ("row", 2), ("row", 1), ("col", 4), ("col", 2), ("col", 1)):
        part = jnp.concatenate([part, swap(part, axis, 8, distance)], 0)

    packed = pack_rows(child_map, ids, messages)
    arrived = lax.all_to_all(packed, ("sib", "row"), 0, 0, tiled=True)
    rows, cols = thin_rows(child_map, ids, arrived)
    cols = lax.all_gather(cols, ("sib", "col"), tiled=True)
    row_pieces = [swap(rows, "row", NROW, d) for d in range(NROW)]
    factors = factor(ids, part, orig_pivot)
    front = assemble(child_map, ids, arrived)
    return update(child_map, ids, front, cols, factors, row_pieces)


def solution(mesh):
    return jax.shard_map(
        body,
        mesh=mesh,
        in_specs=(P("sib", "row", "col"), P(), P()),
        out_specs=P("row", ("sib", "col")),
        check_vma=False,
    )
```

```python
import functools

import jax
import jax.numpy as jnp
from jax import lax
from jax.experimental import pallas as pl
from jax.experimental.pallas import tpu as pltpu
from jax.sharding import PartitionSpec as P

BLK = 128
TILE = 256
NF = 20480
PANELS = 2
FS = PANELS * TILE
NROW = 8
NCOL = 8
PER = 8
FRONT_ROWS = NF // NROW
FRONT_COLS = NF // (2 * NCOL)
ROW_SLOTS = FRONT_ROWS // BLK
THIN = 32 + 8
MSG = THIN + BLK
F32 = jnp.float32
VMEM = pl.BlockSpec(memory_space=pltpu.VMEM)
SMEM = pl.BlockSpec(memory_space=pltpu.SMEM)
LIMIT = 56 * 2**20


def product(left, right):
    return jnp.dot(left, right, precision=lax.Precision.HIGHEST, preferred_element_type=F32)


ROW_PLACE = 0
RANK = 8
HALF = 16
ROW_SLOT = 24
COL_SLOT = 40
PIVOT_ROW = 48
PIVOT_COL = 80
PLAN = 96


def split(value):
    high = value.astype(jnp.bfloat16)
    low = (value - high.astype(F32)).astype(jnp.bfloat16)
    return high, low


def product3(left, right):
    dot = lambda a, b: jnp.dot(a, b, preferred_element_type=F32)
    return dot(left[0], right[0]) + (dot(left[0], right[1]) + dot(left[1], right[0]))


def target(maps, child, line, place):
    return maps[child, 2 * ((place // 2) * NROW + line) + place % 2]


def class_of(block):
    return (block // 2) % NROW


def half_of(block):
    return (block // 2) // NROW % 2


def row_slot(block):
    return 2 * (block // 2 // NROW) + block % 2


def col_slot(block):
    return 2 * (block // 2 // (2 * NCOL)) + block % 2


def place_of(maps, child, line, wanted):
    found = jnp.int32(0)
    block = jnp.int32(0)
    for place in range(PER):
        here = target(maps, child, line, place)
        hit = class_of(here) == wanted
        found = jnp.where(hit, place, found)
        block = jnp.where(hit, here, block)
    return found, block


def at(index, size):
    return pl.ds(pl.multiple_of(index * size, size), size)


def plan_kernel(maps, ids, out):
    sib, row, col = ids[0], ids[1], ids[2]
    for dest in range(NROW):
        out[ROW_PLACE + dest] = place_of(maps, sib, row, dest)[0]
    blocks = [[place_of(maps, child, j, col)[1] for j in range(NCOL)] for child in range(2)]
    for d in range(NCOL):
        source = col ^ d
        block = place_of(maps, sib, source, col)[1]
        half = half_of(block)
        rank = jnp.int32(0)
        for j in range(NCOL):
            here = half_of(jnp.where(sib == 0, blocks[0][j], blocks[1][j])) == half
            rank += jnp.where((j < source) & here, 1, 0)
        out[RANK + d] = rank
        out[HALF + d] = half
        for b in range(PANELS):
            block = place_of(maps, sib, source, b)[1]
            out[PIVOT_COL + PANELS * d + b] = jnp.where(block // 2 == b, block, -1)
    for child in range(2):
        count = jnp.int32(0)
        found = [jnp.int32(0)] * 4
        for j in range(NCOL):
            block = blocks[child][j]
            mine = half_of(block) == sib
            for r in range(4):
                found[r] = jnp.where(mine & (count == r), col_slot(block), found[r])
            count += jnp.where(mine, 1, 0)
        for r in range(4):
            out[COL_SLOT + 4 * child + r] = found[r]
        for line in range(NROW):
            source = child * NROW + line
            out[ROW_SLOT + source] = row_slot(place_of(maps, child, line, row)[1])
            for a in range(PANELS):
                block = place_of(maps, child, line, a)[1]
                out[PIVOT_ROW + PANELS * source + a] = jnp.where(block // 2 == a, block, -1)


def plan(maps, ids):
    return pl.pallas_call(
        plan_kernel,
        out_shape=jax.ShapeDtypeStruct((PLAN,), jnp.int32),
        in_specs=[SMEM, SMEM],
        out_specs=SMEM,
        cost_estimate=pl.CostEstimate(flops=10**7, bytes_accessed=2**10, transcendentals=0),
    )(maps, ids)


def pack_thin_kernel(maps, ids, x_ref, out):
    child, col = ids[0], ids[2]
    for b in range(PANELS):
        q, _ = place_of(maps, child, col, b)
        for dest in range(NCOL):
            for p in range(PER):
                start = p * BLK + dest * 16
                out[dest, b, p * 16 : (p + 1) * 16, :] = x_ref[start : start + 16, at(q, BLK)]


def pack_thin(maps, ids, x):
    return pl.pallas_call(
        pack_thin_kernel,
        out_shape=jax.ShapeDtypeStruct((NCOL, PANELS, BLK, BLK), F32),
        in_specs=[SMEM, SMEM, VMEM],
        out_specs=VMEM,
        compiler_params=pltpu.CompilerParams(vmem_limit_bytes=LIMIT),
        cost_estimate=pl.CostEstimate(flops=0, bytes_accessed=6 * 2**20, transcendentals=0),
    )(maps, ids, x)


def place_thin_kernel(table, ids, in_ref, thin, pivot):
    child, row, col = ids[0], ids[1], ids[2]
    thin[...] = jnp.zeros_like(thin)
    pivot[...] = jnp.zeros_like(pivot)
    for d in range(NCOL):
        for b in range(PANELS):
            block = table[PIVOT_COL + PANELS * d + b]

            @pl.when(block >= 0)
            def _():
                thin[:, at(block, BLK)] = in_ref[col ^ d, b]

    for a in range(PANELS):
        block = table[PIVOT_ROW + PANELS * (child * NROW + row) + a]

        @pl.when(block >= 0)
        def _():
            pivot[at(block, 16), :] = thin[at(table[ROW_PLACE + a], 16), :]


def place_thin(table, ids, arrived):
    return pl.pallas_call(
        place_thin_kernel,
        out_shape=(jax.ShapeDtypeStruct((BLK, FS), F32), jax.ShapeDtypeStruct((FS // NCOL, FS), F32)),
        in_specs=[SMEM, SMEM, VMEM],
        out_specs=(VMEM, VMEM),
        compiler_params=pltpu.CompilerParams(vmem_limit_bytes=LIMIT),
        cost_estimate=pl.CostEstimate(flops=0, bytes_accessed=2 * 2**20, transcendentals=0),
    )(table, ids, arrived)


def pack_cols_kernel(maps, ids, x_ref, *out_refs):
    for d in range(NCOL):
        q, _ = place_of(maps, ids[0], ids[2], ids[2] ^ d)
        out_refs[d][...] = x_ref[:, at(q, BLK)]


def pack_cols(maps, ids, x):
    message = jax.ShapeDtypeStruct((PER * BLK, BLK), F32)
    return pl.pallas_call(
        pack_cols_kernel,
        out_shape=[message] * NCOL,
        in_specs=[SMEM, SMEM, VMEM],
        out_specs=[VMEM] * NCOL,
        compiler_params=pltpu.CompilerParams(vmem_limit_bytes=LIMIT),
        cost_estimate=pl.CostEstimate(flops=0, bytes_accessed=10 * 2**20, transcendentals=0),
    )(maps, ids, x)


def pack_rows_kernel(table, thin, *refs):
    in_refs, out = refs[:NCOL], refs[NCOL]
    dest = pl.program_id(0)
    place = table[ROW_PLACE + dest]
    for d in range(NCOL):
        half = table[HALF + d]
        lanes = at(table[RANK + d], BLK)
        out[half, 0, THIN:, lanes] = in_refs[d][at(place, BLK), :]
        for a in range(PANELS):
            start = table[ROW_PLACE + a] * BLK + dest * 16
            out[half, 0, 16 * a : 16 * (a + 1), lanes] = in_refs[d][
                pl.ds(pl.multiple_of(start, 16), 16), :
            ]
    for half in range(2):
        out[half, 0, 32:THIN, :] = thin[pl.ds(pl.multiple_of(place * 16 + half * 8, 8), 8), :]


def pack_rows(table, thin, pieces):
    return pl.pallas_call(
        pack_rows_kernel,
        grid=(NROW,),
        out_shape=jax.ShapeDtypeStruct((2, NROW, MSG, FS), F32),
        in_specs=[SMEM] + [VMEM] * (1 + NCOL),
        out_specs=pl.BlockSpec((2, 1, MSG, FS), lambda i: (0, i, 0, 0)),
        compiler_params=pltpu.CompilerParams(vmem_limit_bytes=LIMIT),
        cost_estimate=pl.CostEstimate(flops=0, bytes_accessed=10 * 2**20, transcendentals=0),
    )(table, thin, *pieces)


def thin_rows_kernel(table, in_ref, rows_ref, cols_ref):
    rows_ref[...] = jnp.zeros_like(rows_ref)
    for source in range(2 * NROW):
        cols_ref[source * 8 : (source + 1) * 8, :] = in_ref[source, 32:, :]
        for a in range(PANELS):
            block = table[PIVOT_ROW + PANELS * source + a]

            @pl.when(block >= 0)
            def _():
                start = source // NROW * 64 + block * 16
                rows_ref[pl.ds(pl.multiple_of(start, 16), 16), :] = in_ref[
                    source, 16 * a : 16 * (a + 1), :
                ]


def thin_rows(table, arrived):
    out = jax.ShapeDtypeStruct((BLK, FS), F32)
    whole = pl.BlockSpec((BLK, FS), lambda i: (0, 0))
    return pl.pallas_call(
        thin_rows_kernel,
        grid=(1,),
        out_shape=(out, out),
        in_specs=[SMEM, pl.BlockSpec((2 * NROW, THIN, FS), lambda i: (0, 0, 0))],
        out_specs=(whole, whole),
        compiler_params=pltpu.CompilerParams(vmem_limit_bytes=LIMIT),
        cost_estimate=pl.CostEstimate(flops=0, bytes_accessed=2 * 2**20, transcendentals=0),
    )(table, arrived)


def invert_block(a, rows, cols):
    n = BLK
    lane8 = lax.broadcasted_iota(jnp.int32, (8, n), 1)
    row8 = lax.broadcasted_iota(jnp.int32, (8, n), 0)
    lane_rest = lax.broadcasted_iota(jnp.int32, (n - 8, n), 1)

    def across(x, j):
        return jnp.broadcast_to(x[:, j : j + 1], x.shape)

    def down(x, j):
        return jnp.broadcast_to(x[j : j + 1, :], x.shape)

    def group(g, s):
        top = s[:8]
        side = s[:, :8].T
        tops = [across(top, j) for j in range(8)]
        sides = [across(side, j) for j in range(8)]
        upper, lower = [], []
        for t in range(8):
            inv = 1.0 / down(tops[t], t)
            upper.append(top[t : t + 1, :])
            r = jnp.where(lane8 == t, 1.0, down(top, t)) * inv
            c = down(side, t)
            lower.append((c * inv)[0:1, :])
            rho = sides[t] * inv
            top = jnp.where(row8 == t, r, jnp.where(lane8 == t, 0.0, top) - tops[t] * r)
            side = jnp.where(lane8 == t, rho, side - rho * c)
            for j in range(t + 1, 8):
                scaled = down(tops[j], t) * inv
                tops[j] = jnp.where(row8 == t, scaled, tops[j] - tops[t] * scaled)
                sides[j] = sides[j] - down(sides[j], t) * rho
        rows[at(g, 8), :] = pltpu.roll(jnp.concatenate(upper, 0), g * 8, 1)
        cols[at(g, 8), :] = pltpu.roll(jnp.concatenate(lower, 0), g * 8, 1)
        rest = s[8:]
        new = jnp.where(lane_rest < 8, 0.0, rest)
        for j in range(8):
            new = new - across(rest, j) * jnp.broadcast_to(top[j : j + 1, :], rest.shape)
        return pltpu.roll(jnp.concatenate([new, top], 0), n - 8, 1)

    inverse = lax.fori_loop(0, n // 8, group, a)
    row = lax.broadcasted_iota(jnp.int32, (n, n), 0)
    lane = lax.broadcasted_iota(jnp.int32, (n, n), 1)
    eye = row == lane
    upper = rows[...]
    lower = cols[...].T
    packed = jnp.where(row > lane, lower, upper)
    lower_inv = jnp.where(row > lane, upper, jnp.where(eye, 1.0, 0.0))
    upper_inv = jnp.where(row < lane, -lower, jnp.where(eye, 1.0 / upper, 0.0))
    return inverse, packed, lower_inv, upper_inv


def eliminate(k, inv_ref, linv_ref, uinv_ref, lu_ref, rows, cols):
    count, n = FS // BLK, BLK
    lo, hi = k * n, (k + 1) * n
    inverse, packed, lower_inv, upper_inv = invert_block(inv_ref[lo:hi, lo:hi], rows, cols)
    x = inv_ref[lo:hi, :]
    y = inv_ref[:, lo:hi]
    scaled_rows = product(lower_inv, x)
    scaled_cols = product(y, upper_inv)
    lu_ref[lo:hi, lo:hi] = packed
    linv_ref[lo:hi, lo:hi] = lower_inv
    uinv_ref[lo:hi, lo:hi] = upper_inv
    if k > 0:
        linv_ref[lo:hi, :lo] = scaled_rows[:, :lo]
        uinv_ref[:lo, lo:hi] = -scaled_cols[:lo]
    if k < count - 1:
        lu_ref[lo:hi, hi:] = scaled_rows[:, hi:]
        lu_ref[hi:, lo:hi] = scaled_cols[hi:]
    inv_ref[lo:hi, :] = product(inverse, x)
    inv_ref[lo:hi, lo:hi] = inverse
    x = inv_ref[lo:hi, :]
    for i in range(count):
        if i != k:
            a, b = i * n, (i + 1) * n
            inv_ref[a:b, lo:hi] = jnp.zeros((n, n), F32)
            inv_ref[a:b, :] = inv_ref[a:b, :] - product(y[a:b], x)


def factor_first_kernel(ids, pieces_ref, orig_ref, inv_ref, linv_ref, uinv_ref, lu_ref, rows, cols):
    inv_ref[...] = orig_ref[...]
    for q in range(NCOL):
        owner = ids[2] ^ (4 * (q & 1) + (q & 2) + (q >> 2 & 1))
        for b in range(FS // BLK):
            start = q * (FS // NCOL) + b * 16
            place = pl.ds(pl.multiple_of(b * BLK + owner * 16, 16), 16)
            inv_ref[place, :] += pieces_ref[start : start + 16, :]
    linv_ref[...] = jnp.zeros_like(linv_ref)
    uinv_ref[...] = jnp.zeros_like(uinv_ref)
    lu_ref[...] = jnp.zeros_like(lu_ref)
    eliminate(0, inv_ref, linv_ref, uinv_ref, lu_ref, rows, cols)


def factor_next_kernel(steps, *refs):
    sources, dests, (rows, cols) = refs[:4], refs[4:8], refs[8:]
    for source, dest in zip(sources, dests):
        dest[...] = source[...]
    for k in steps:
        eliminate(k, *dests, rows, cols)


def factor(kernel, specs, flops, *operands):
    square = jax.ShapeDtypeStruct((FS, FS), F32)
    return pl.pallas_call(
        kernel,
        out_shape=(square,) * 4,
        in_specs=specs,
        out_specs=(VMEM,) * 4,
        scratch_shapes=[pltpu.VMEM((BLK, BLK), F32)] * 2,
        compiler_params=pltpu.CompilerParams(vmem_limit_bytes=LIMIT),
        cost_estimate=pl.CostEstimate(flops=flops, bytes_accessed=6 * 2**20, transcendentals=0),
    )(*operands)


def update_kernel(table, ids, arrived_ref, inv_ref, linv_ref, uinv_ref, lu_ref, *refs):
    col_refs, row_refs, out_ref = refs[:NCOL], refs[NCOL : NCOL + 4], refs[NCOL + 4]
    left, left_parts, right_parts, pivots = refs[NCOL + 5 :]
    step = pl.program_id(0)
    sib, row, col = ids[0], ids[1], ids[2]
    group = sib * NCOL + col

    @pl.when(step == 0)
    def _():
        pivots[...] = jnp.zeros_like(pivots)
        for child in range(2):
            for r in range(4):
                lanes = at(table[COL_SLOT + 4 * child + r], BLK)
                for d in range(NROW):
                    for b in range(4):
                        start = (d // 4) * BLK + child * 64 + b * 16
                        rows = pl.ds(pl.multiple_of(b * BLK + (row ^ d) * 16, 16), 16)
                        pivots[rows, lanes] += row_refs[d % 4][
                            start : start + 16, r * BLK : (r + 1) * BLK
                        ]
        high, low = split(product3(split(-inv_ref[...]), split(pivots[...])))
        right_parts[:FS] = high
        right_parts[FS : 2 * FS] = low
        right_parts[2 * FS :] = high

    left[...] = jnp.zeros_like(left)
    for source in range(2 * NROW):
        slot = table[ROW_SLOT + source]

        @pl.when(slot // 2 == step)
        def _():
            for d in range(NCOL):
                for ds in range(2):
                    start = slot % 2 * BLK + (col ^ d) * 16 + (sib ^ ds) * 8
                    left[pl.ds(pl.multiple_of(start, 8), 8), :] += col_refs[d][
                        ds * BLK + source * 8 : ds * BLK + source * 8 + 8, :
                    ]

    high, low = split(left[...])
    left_parts[:, :FS] = high
    left_parts[:, FS : 2 * FS] = high
    left_parts[:, 2 * FS :] = low
    out_ref[...] = jnp.dot(left_parts[...], right_parts[...], preferred_element_type=F32)

    for source in range(2 * NROW):
        slot = table[ROW_SLOT + source]

        @pl.when(slot // 2 == step)
        def _():
            rows = at(slot % 2, BLK)
            for r in range(4):
                lanes = at(table[COL_SLOT + source // NROW * 4 + r], BLK)
                out_ref[rows, lanes] += arrived_ref[source, THIN:, r * BLK : (r + 1) * BLK]

    @pl.when(group < PANELS)
    def _():
        out_ref[:, :TILE] = product(left[...], uinv_ref[:, at(group, TILE)])

    @pl.when((step == 0) & (row < PANELS))
    def _():
        out_ref[...] = product(linv_ref[at(row, TILE), :], pivots[...])

        @pl.when(group < PANELS)
        def _():
            out_ref[:, :TILE] = lu_ref[at(row, TILE), at(group, TILE)]


def update(table, ids, arrived, factors, col_pieces, row_pieces):
    return pl.pallas_call(
        update_kernel,
        grid=(FRONT_ROWS // TILE,),
        out_shape=jax.ShapeDtypeStruct((FRONT_ROWS, FRONT_COLS), F32),
        in_specs=[SMEM, SMEM] + [VMEM] * (1 + 4 + NCOL + 4),
        out_specs=pl.BlockSpec((TILE, FRONT_COLS), lambda i: (i, 0)),
        scratch_shapes=[
            pltpu.VMEM((TILE, FS), F32),
            pltpu.VMEM((TILE, 3 * FS), jnp.bfloat16),
            pltpu.VMEM((3 * FS, FRONT_COLS), jnp.bfloat16),
            pltpu.VMEM((FS, FRONT_COLS), F32),
        ],
        compiler_params=pltpu.CompilerParams(vmem_limit_bytes=LIMIT),
        cost_estimate=pl.CostEstimate(
            flops=6 * FRONT_ROWS * FRONT_COLS * FS, bytes_accessed=30 * 2**20, transcendentals=0
        ),
    )(table, ids, arrived, *factors, *col_pieces, *row_pieces)


def swap(value, axis, size, distance):
    if distance == 0:
        return value
    return lax.ppermute(value, axis, [(i, i ^ distance) for i in range(size)])


def tie(*values):
    return lax.optimization_barrier(values)


def body(child_upd, child_map, orig_pivot):
    ids = jnp.stack([lax.axis_index("sib"), lax.axis_index("row"), lax.axis_index("col")])
    ids = ids.astype(jnp.int32)
    x = child_upd[0]
    table = plan(child_map, ids)
    thin = pack_thin(child_map, ids, x)
    thin = lax.all_to_all(thin, "col", 0, 0, tiled=True)
    thin, x = tie(thin, x)
    thin, part = place_thin(table, ids, thin)

    messages = list(pack_cols(child_map, ids, x))
    order = (4, 6, 2, 5, 7, 3, 1)
    rounds = [("sib", 1), ("row", 4), ("row", 1), ("row", 2), ("col", 4), ("col", 2), ("col", 1)]
    for d, (axis, distance) in zip(order, rounds):
        other = swap(part, axis, 2 if axis == "sib" else 8, distance)
        part = jnp.concatenate([part, other], 0) if axis == "col" else part + other
        messages[d], part = tie(swap(messages[d], "col", NCOL, d), part)

    packed = pack_rows(table, thin, messages).reshape(2 * NROW, MSG, FS)
    packed, part = tie(packed, part)
    arrived = lax.all_to_all(packed, ("sib", "row"), 0, 0, tiled=True)
    rows, cols = thin_rows(table, arrived)

    cols = jnp.concatenate([cols, swap(cols, "sib", 2, 1)], 0)
    rows = jnp.concatenate([rows, swap(rows, "row", NROW, 4)], 0)
    four = [VMEM] * 4
    factors = factor(factor_first_kernel, [SMEM, VMEM, VMEM], 10**10, ids, part, orig_pivot)
    cols, rows, factors = tie(cols, rows, factors)
    c, r = {0: cols}, {0: rows}
    for d in (1, 3):
        c[2 * d], r[d] = swap(cols, "col", NCOL, 2 * d), swap(rows, "row", NROW, d)
    factors = factor(functools.partial(factor_next_kernel, (1,)), four, 10**10, *factors)
    c, r, cols, rows, factors = tie(c, r, cols, rows, factors)
    c[4], r[2] = swap(cols, "col", NCOL, 4), swap(rows, "row", NROW, 2)
    for d in (0, 2, 6):
        c[d + 1] = swap(c[d], "col", NCOL, 1)
    factors = factor(functools.partial(factor_next_kernel, (2, 3)), four, 2 * 10**10, *factors)
    c, r, factors = tie(c, r, factors)
    c[5] = swap(c[4], "col", NCOL, 1)
    return update(
        table, ids, arrived, factors, [c[d] for d in range(NCOL)], [r[d] for d in range(4)]
    )


def solution(mesh):
    return jax.shard_map(
        body,
        mesh=mesh,
        in_specs=(P("sib", "row", "col"), P(), P()),
        out_specs=P("row", ("sib", "col")),
        check_vma=False,
    )
```

```python
import functools

import jax
import jax.numpy as jnp
from jax import lax
from jax.experimental import pallas as pl
from jax.experimental.pallas import tpu as pltpu
from jax.sharding import PartitionSpec as P

BLK = 128
TILE = 256
NF = 20480
PANELS = 2
FS = PANELS * TILE
NROW = 8
NCOL = 8
PER = 8
FRONT_ROWS = NF // NROW
FRONT_COLS = NF // (2 * NCOL)
ROW_SLOTS = FRONT_ROWS // BLK
HALF_BLK = BLK // 2
THIN = (40, 0)
F32 = jnp.float32
VMEM = pl.BlockSpec(memory_space=pltpu.VMEM)
SMEM = pl.BlockSpec(memory_space=pltpu.SMEM)
ANY = pl.BlockSpec(memory_space=pl.ANY)
SPAN = 2 * TILE
LIMIT = 56 * 2**20


def product(left, right):
    return jnp.dot(left, right, precision=lax.Precision.HIGHEST, preferred_element_type=F32)


ROW_PLACE = 0
RANK = 8
HALF = 16
ROW_SLOT = 24
COL_SLOT = 40
PIVOT_ROW = 48
PIVOT_COL = 80
PLAN = 96


def split(value):
    high = value.astype(jnp.bfloat16)
    low = (value - high.astype(F32)).astype(jnp.bfloat16)
    return high, low


def product3(left, right):
    dot = lambda a, b: jnp.dot(a, b, preferred_element_type=F32)
    return dot(left[0], right[0]) + (dot(left[0], right[1]) + dot(left[1], right[0]))


def target(maps, child, line, place):
    return maps[child, 2 * ((place // 2) * NROW + line) + place % 2]


def class_of(block):
    return (block // 2) % NROW


def half_of(block):
    return (block // 2) // NROW % 2


def row_slot(block):
    return 2 * (block // 2 // NROW) + block % 2


def col_slot(block):
    return 2 * (block // 2 // (2 * NCOL)) + block % 2


def place_of(maps, child, line, wanted):
    found = jnp.int32(0)
    block = jnp.int32(0)
    for place in range(PER):
        here = target(maps, child, line, place)
        hit = class_of(here) == wanted
        found = jnp.where(hit, place, found)
        block = jnp.where(hit, here, block)
    return found, block


def at(index, size):
    return pl.ds(pl.multiple_of(index * size, size), size)


def plan_kernel(maps, ids, out):
    sib, row, col = ids[0], ids[1], ids[2]
    for dest in range(NROW):
        out[ROW_PLACE + dest] = place_of(maps, sib, row, dest)[0]
    blocks = [[place_of(maps, child, j, col)[1] for j in range(NCOL)] for child in range(2)]
    for d in range(NCOL):
        source = col ^ d
        block = place_of(maps, sib, source, col)[1]
        half = half_of(block)
        rank = jnp.int32(0)
        for j in range(NCOL):
            here = half_of(jnp.where(sib == 0, blocks[0][j], blocks[1][j])) == half
            rank += jnp.where((j < source) & here, 1, 0)
        out[RANK + d] = rank
        out[HALF + d] = half
        for b in range(PANELS):
            block = place_of(maps, sib, source, b)[1]
            out[PIVOT_COL + PANELS * d + b] = jnp.where(block // 2 == b, block, -1)
    for child in range(2):
        count = jnp.int32(0)
        found = [jnp.int32(0)] * 4
        for j in range(NCOL):
            block = blocks[child][j]
            mine = half_of(block) == sib
            for r in range(4):
                found[r] = jnp.where(mine & (count == r), col_slot(block), found[r])
            count += jnp.where(mine, 1, 0)
        for r in range(4):
            out[COL_SLOT + 4 * child + r] = found[r]
        for line in range(NROW):
            source = child * NROW + line
            out[ROW_SLOT + source] = row_slot(place_of(maps, child, line, row)[1])
            for a in range(PANELS):
                block = place_of(maps, child, line, a)[1]
                out[PIVOT_ROW + PANELS * source + a] = jnp.where(block // 2 == a, block, -1)


def plan(maps, ids):
    return pl.pallas_call(
        plan_kernel,
        out_shape=jax.ShapeDtypeStruct((PLAN,), jnp.int32),
        in_specs=[SMEM, SMEM],
        out_specs=SMEM,
        cost_estimate=pl.CostEstimate(flops=10**7, bytes_accessed=2**10, transcendentals=0),
    )(maps, ids)


def pack_thin_kernel(maps, ids, x_ref, out):
    child, col = ids[0], ids[2]
    for b in range(PANELS):
        q, _ = place_of(maps, child, col, b)
        for dest in range(NCOL):
            for p in range(PER):
                start = p * BLK + dest * 16
                out[dest, b, p * 16 : (p + 1) * 16, :] = x_ref[start : start + 16, at(q, BLK)]


def pack_thin(maps, ids, x):
    return pl.pallas_call(
        pack_thin_kernel,
        out_shape=jax.ShapeDtypeStruct((NCOL, PANELS, BLK, BLK), F32),
        in_specs=[SMEM, SMEM, VMEM],
        out_specs=VMEM,
        compiler_params=pltpu.CompilerParams(vmem_limit_bytes=LIMIT),
        cost_estimate=pl.CostEstimate(flops=0, bytes_accessed=6 * 2**20, transcendentals=0),
    )(maps, ids, x)


def place_thin_kernel(table, ids, in_ref, thin, pivot):
    child, row, col = ids[0], ids[1], ids[2]
    thin[...] = jnp.zeros_like(thin)
    pivot[...] = jnp.zeros_like(pivot)
    for d in range(NCOL):
        for b in range(PANELS):
            block = table[PIVOT_COL + PANELS * d + b]

            @pl.when(block >= 0)
            def _():
                thin[:, at(block, BLK)] = in_ref[col ^ d, b]

    for a in range(PANELS):
        block = table[PIVOT_ROW + PANELS * (child * NROW + row) + a]

        @pl.when(block >= 0)
        def _():
            pivot[at(block, 16), :] = thin[at(table[ROW_PLACE + a], 16), :]


def place_thin(table, ids, arrived):
    return pl.pallas_call(
        place_thin_kernel,
        out_shape=(jax.ShapeDtypeStruct((BLK, FS), F32), jax.ShapeDtypeStruct((FS // NCOL, FS), F32)),
        in_specs=[SMEM, SMEM, VMEM],
        out_specs=(VMEM, VMEM),
        compiler_params=pltpu.CompilerParams(vmem_limit_bytes=LIMIT),
        cost_estimate=pl.CostEstimate(flops=0, bytes_accessed=2 * 2**20, transcendentals=0),
    )(table, ids, arrived)


def pack_first_cols_kernel(maps, ids, x_ref, *out_refs):
    others = [place_of(maps, ids[0], ids[1], a)[0] for a in range(PANELS)]
    for d in range(NCOL):
        lanes = at(place_of(maps, ids[0], ids[2], ids[2] ^ d)[0], BLK)
        out_refs[d][:PER] = x_ref[:, :HALF_BLK, lanes]
        for a in range(PANELS):
            out_refs[d][PER + a] = x_ref[others[a], HALF_BLK:, lanes]


def pack_second_cols_kernel(maps, ids, x_ref, *out_refs):
    others = [place_of(maps, ids[0], ids[1], a)[0] for a in range(PANELS, NROW)]
    for d in range(NCOL):
        lanes = at(place_of(maps, ids[0], ids[2], ids[2] ^ d)[0], BLK)
        for a in range(NROW - PANELS):
            out_refs[d][a] = x_ref[others[a], :, lanes]


def pack_cols(maps, ids, x, part):
    kernel = (pack_first_cols_kernel, pack_second_cols_kernel)[part]
    shape = ((PER + PANELS, PER - PANELS)[part], HALF_BLK, BLK)
    return pl.pallas_call(
        kernel,
        grid=(1,),
        out_shape=[jax.ShapeDtypeStruct(shape, F32)] * NCOL,
        in_specs=[
            SMEM,
            SMEM,
            pl.BlockSpec((PER, (BLK, HALF_BLK)[part], PER * BLK), lambda i: (0, part, 0)),
        ],
        out_specs=[pl.BlockSpec(shape, lambda i: (0, 0, 0))] * NCOL,
        compiler_params=pltpu.CompilerParams(vmem_limit_bytes=LIMIT),
        cost_estimate=pl.CostEstimate(flops=0, bytes_accessed=5 * 2**20, transcendentals=0),
    )(maps, ids, x.reshape(PER, BLK, PER * BLK))


def pack_first_kernel(table, thin, *refs):
    in_refs, out = refs[:NCOL], refs[NCOL]
    dest = pl.program_id(0)
    place = table[ROW_PLACE + dest]
    rows = at(dest % 4, 16)
    for d in range(NCOL):
        half, lanes = table[HALF + d], at(table[RANK + d], BLK)
        out[half, 0, THIN[0] :, lanes] = in_refs[d][place]
        for a in range(PANELS):
            source = jnp.where(dest < 4, table[ROW_PLACE + a], PER + a)
            out[half, 0, 8 + 16 * a : 24 + 16 * a, lanes] = in_refs[d][source, rows, :]
    for half in range(2):
        out[half, 0, :8, :] = thin[pl.ds(pl.multiple_of(place * 16 + half * 8, 8), 8), :]


def pack_second_kernel(table, *refs):
    first_refs, in_refs, out = refs[:NCOL], refs[NCOL : 2 * NCOL], refs[2 * NCOL]
    dest = pl.program_id(0)
    for d in range(NCOL):
        half, lanes = table[HALF + d], at(table[RANK + d], BLK)

        @pl.when(dest < PANELS)
        def _():
            out[half, 0, :, lanes] = first_refs[d][jnp.minimum(PER + dest, PER + PANELS - 1)]

        @pl.when(dest >= PANELS)
        def _():
            out[half, 0, :, lanes] = in_refs[d][jnp.maximum(dest - PANELS, 0)]


def pack_rows(part, table, *pieces):
    height = THIN[part] + HALF_BLK
    return pl.pallas_call(
        (pack_first_kernel, pack_second_kernel)[part],
        grid=(NROW,),
        out_shape=jax.ShapeDtypeStruct((2, NROW, height, FS), F32),
        in_specs=[SMEM] + [VMEM] * len(pieces),
        out_specs=pl.BlockSpec((2, 1, height, FS), lambda i: (0, i, 0, 0)),
        compiler_params=pltpu.CompilerParams(vmem_limit_bytes=LIMIT),
        cost_estimate=pl.CostEstimate(flops=0, bytes_accessed=6 * 2**20, transcendentals=0),
    )(table, *pieces).reshape(2 * NROW, height, FS)


def thin_rows_kernel(table, in_ref, rows_ref, cols_ref):
    rows_ref[...] = jnp.zeros_like(rows_ref)
    for source in range(2 * NROW):
        cols_ref[source * 8 : (source + 1) * 8, :] = in_ref[source, :8, :]
        for a in range(PANELS):
            block = table[PIVOT_ROW + PANELS * source + a]

            @pl.when(block >= 0)
            def _():
                start = source // NROW * 64 + block * 16
                rows_ref[pl.ds(pl.multiple_of(start, 16), 16), :] = in_ref[
                    source, 8 + 16 * a : 24 + 16 * a, :
                ]


def thin_rows(table, arrived):
    out = jax.ShapeDtypeStruct((BLK, FS), F32)
    whole = pl.BlockSpec((BLK, FS), lambda i: (0, 0))
    return pl.pallas_call(
        thin_rows_kernel,
        grid=(1,),
        out_shape=(out, out),
        in_specs=[SMEM, pl.BlockSpec((2 * NROW, THIN[0], FS), lambda i: (0, 0, 0))],
        out_specs=(whole, whole),
        compiler_params=pltpu.CompilerParams(vmem_limit_bytes=LIMIT),
        cost_estimate=pl.CostEstimate(flops=0, bytes_accessed=2 * 2**20, transcendentals=0),
    )(table, arrived)


def invert_block(a, rows, cols):
    n = BLK
    lane8 = lax.broadcasted_iota(jnp.int32, (8, n), 1)
    row8 = lax.broadcasted_iota(jnp.int32, (8, n), 0)
    lane_rest = lax.broadcasted_iota(jnp.int32, (n - 8, n), 1)

    def across(x, j):
        return jnp.broadcast_to(x[:, j : j + 1], x.shape)

    def down(x, j):
        return jnp.broadcast_to(x[j : j + 1, :], x.shape)

    def group(g, s):
        top = s[:8]
        side = s[:, :8].T
        tops = [across(top, j) for j in range(8)]
        sides = [across(side, j) for j in range(8)]
        upper, lower = [], []
        for t in range(8):
            inv = 1.0 / down(tops[t], t)
            upper.append(top[t : t + 1, :])
            r = jnp.where(lane8 == t, 1.0, down(top, t)) * inv
            c = down(side, t)
            lower.append((c * inv)[0:1, :])
            rho = sides[t] * inv
            top = jnp.where(row8 == t, r, jnp.where(lane8 == t, 0.0, top) - tops[t] * r)
            side = jnp.where(lane8 == t, rho, side - rho * c)
            for j in range(t + 1, 8):
                scaled = down(tops[j], t) * inv
                tops[j] = jnp.where(row8 == t, scaled, tops[j] - tops[t] * scaled)
                sides[j] = sides[j] - down(sides[j], t) * rho
        rows[at(g, 8), :] = pltpu.roll(jnp.concatenate(upper, 0), g * 8, 1)
        cols[at(g, 8), :] = pltpu.roll(jnp.concatenate(lower, 0), g * 8, 1)
        rest = s[8:]
        new = jnp.where(lane_rest < 8, 0.0, rest)
        for j in range(8):
            new = new - across(rest, j) * jnp.broadcast_to(top[j : j + 1, :], rest.shape)
        return pltpu.roll(jnp.concatenate([new, top], 0), n - 8, 1)

    inverse = lax.fori_loop(0, n // 8, group, a)
    row = lax.broadcasted_iota(jnp.int32, (n, n), 0)
    lane = lax.broadcasted_iota(jnp.int32, (n, n), 1)
    eye = row == lane
    upper = rows[...]
    lower = cols[...].T
    packed = jnp.where(row > lane, lower, upper)
    lower_inv = jnp.where(row > lane, upper, jnp.where(eye, 1.0, 0.0))
    upper_inv = jnp.where(row < lane, -lower, jnp.where(eye, 1.0 / upper, 0.0))
    return inverse, packed, lower_inv, upper_inv


def eliminate(k, inv_ref, linv_ref, uinv_ref, lu_ref, rows, cols):
    count, n = FS // BLK, BLK
    lo, hi = k * n, (k + 1) * n
    inverse, packed, lower_inv, upper_inv = invert_block(inv_ref[lo:hi, lo:hi], rows, cols)
    x = inv_ref[lo:hi, :]
    y = inv_ref[:, lo:hi]
    scaled_rows = product(lower_inv, x)
    scaled_cols = product(y, upper_inv)
    lu_ref[lo:hi, lo:hi] = packed
    linv_ref[lo:hi, lo:hi] = lower_inv
    uinv_ref[lo:hi, lo:hi] = upper_inv
    if k > 0:
        linv_ref[lo:hi, :lo] = scaled_rows[:, :lo]
        uinv_ref[:lo, lo:hi] = -scaled_cols[:lo]
    if k < count - 1:
        lu_ref[lo:hi, hi:] = scaled_rows[:, hi:]
        lu_ref[hi:, lo:hi] = scaled_cols[hi:]
    inv_ref[lo:hi, :] = product(inverse, x)
    inv_ref[lo:hi, lo:hi] = inverse
    x = inv_ref[lo:hi, :]
    for i in range(count):
        if i != k:
            a, b = i * n, (i + 1) * n
            inv_ref[a:b, lo:hi] = jnp.zeros((n, n), F32)
            inv_ref[a:b, :] = inv_ref[a:b, :] - product(y[a:b], x)


def factor_first_kernel(ids, pieces_ref, orig_ref, inv_ref, linv_ref, uinv_ref, lu_ref, rows, cols):
    inv_ref[...] = orig_ref[...]
    for q in range(NCOL):
        owner = ids[2] ^ (4 * (q & 1) + (q & 2) + (q >> 2 & 1))
        for b in range(FS // BLK):
            start = q * (FS // NCOL) + b * 16
            place = pl.ds(pl.multiple_of(b * BLK + owner * 16, 16), 16)
            inv_ref[place, :] += pieces_ref[start : start + 16, :]
    linv_ref[...] = jnp.zeros_like(linv_ref)
    uinv_ref[...] = jnp.zeros_like(uinv_ref)
    lu_ref[...] = jnp.zeros_like(lu_ref)
    eliminate(0, inv_ref, linv_ref, uinv_ref, lu_ref, rows, cols)


def factor_next_kernel(steps, *refs):
    sources, dests, (rows, cols) = refs[:4], refs[4:8], refs[8:]
    for source, dest in zip(sources, dests):
        dest[...] = source[...]
    for k in steps:
        eliminate(k, *dests, rows, cols)


def factor(kernel, specs, flops, *operands):
    square = jax.ShapeDtypeStruct((FS, FS), F32)
    return pl.pallas_call(
        kernel,
        out_shape=(square,) * 4,
        in_specs=specs,
        out_specs=(VMEM,) * 4,
        scratch_shapes=[pltpu.VMEM((BLK, BLK), F32)] * 2,
        compiler_params=pltpu.CompilerParams(vmem_limit_bytes=LIMIT),
        cost_estimate=pl.CostEstimate(flops=flops, bytes_accessed=6 * 2**20, transcendentals=0),
    )(*operands)


def update_kernel(table, ids, inv_ref, *refs):
    row_refs, linv_hbm, uinv_hbm, lu_hbm, arrived_hbm = refs[:4], *refs[4:7], refs[7:9]
    col_hbm, out_ref, scratch = refs[9 : 9 + NCOL], refs[9 + NCOL], refs[10 + NCOL :]
    left, left_parts, right_parts, pivots, cols, own, part, sems = scratch
    step = pl.program_id(0)
    sib, row, col = ids[0], ids[1], ids[2]
    group = sib * NCOL + col
    own_copies = [
        pltpu.make_async_copy(
            arrived_hbm[n].at[:, THIN[n] :], own.at[:, at(n, HALF_BLK)], sems.at[NCOL + n]
        )
        for n in range(2)
    ]
    col_copies = [
        pltpu.make_async_copy(col_hbm[d], cols.at[d], sems.at[d]) for d in range(NCOL)
    ]
    part_sem = sems.at[NCOL + 2]

    @pl.when(step == 0)
    def _():
        for copy in col_copies + own_copies:
            copy.start()
        pivots[...] = jnp.zeros_like(pivots)
        for child in range(2):
            for r in range(4):
                lanes = at(table[COL_SLOT + 4 * child + r], BLK)
                for d in range(NROW):
                    for b in range(4):
                        start = (d // 4) * BLK + child * 64 + b * 16
                        rows = pl.ds(pl.multiple_of(b * BLK + (row ^ d) * 16, 16), 16)
                        pivots[rows, lanes] += row_refs[d % 4][
                            start : start + 16, r * BLK : (r + 1) * BLK
                        ]
        high, low = split(product3(split(-inv_ref[...]), split(pivots[...])))
        right_parts[:FS] = high
        right_parts[FS : 2 * FS] = low
        right_parts[2 * FS :] = high
        for copy in col_copies:
            copy.wait()

    left[...] = jnp.zeros_like(left)
    for source in range(2 * NROW):
        slot = table[ROW_SLOT + source]

        @pl.when(slot * BLK // SPAN == step)
        def _():
            for d in range(NCOL):
                for ds in range(2):
                    start = slot * BLK % SPAN + (col ^ d) * 16 + (sib ^ ds) * 8
                    left[pl.ds(pl.multiple_of(start, 8), 8), :] += cols[
                        d, ds * BLK + source * 8 : ds * BLK + source * 8 + 8, :
                    ]

    high, low = split(left[...])
    left_parts[:, :FS] = high
    left_parts[:, FS : 2 * FS] = high
    left_parts[:, 2 * FS :] = low
    out_ref[...] = jnp.dot(left_parts[...], right_parts[...], preferred_element_type=F32)

    @pl.when(step == 0)
    def _():
        for copy in own_copies:
            copy.wait()

    for source in range(2 * NROW):
        slot = table[ROW_SLOT + source]

        @pl.when(slot * BLK // SPAN == step)
        def _():
            rows = at(slot * BLK % SPAN // BLK, BLK)
            for r in range(4):
                lanes = at(table[COL_SLOT + source // NROW * 4 + r], BLK)
                out_ref[rows, lanes] += own[source, :, r * BLK : (r + 1) * BLK]

    @pl.when(group < PANELS)
    def _():
        copy = pltpu.make_async_copy(uinv_hbm, part, part_sem)
        copy.start()
        copy.wait()
        out_ref[:, :TILE] = product(left[...], part[:, at(group, TILE)])

    @pl.when((step == 0) & (row < PANELS))
    def _():
        copy = pltpu.make_async_copy(linv_hbm, part, part_sem)
        copy.start()
        copy.wait()
        out_ref[:TILE] = product(part[at(row, TILE), :], pivots[...])

        @pl.when(group < PANELS)
        def _():
            copy = pltpu.make_async_copy(lu_hbm, part, part_sem)
            copy.start()
            copy.wait()
            out_ref[:TILE, :TILE] = part[at(row, TILE), at(group, TILE)]


def update(table, ids, arrived, factors, col_pieces, row_pieces):
    inverse, *others = factors
    return pl.pallas_call(
        update_kernel,
        grid=(FRONT_ROWS // SPAN,),
        out_shape=jax.ShapeDtypeStruct((FRONT_ROWS, FRONT_COLS), F32),
        in_specs=[SMEM, SMEM] + [VMEM] * 5 + [ANY] * (5 + NCOL),
        out_specs=pl.BlockSpec((SPAN, FRONT_COLS), lambda i: (i, 0)),
        scratch_shapes=[
            pltpu.VMEM((SPAN, FS), F32),
            pltpu.VMEM((SPAN, 3 * FS), jnp.bfloat16),
            pltpu.VMEM((3 * FS, FRONT_COLS), jnp.bfloat16),
            pltpu.VMEM((FS, FRONT_COLS), F32),
            pltpu.VMEM((NCOL, 2 * BLK, FS), F32),
            pltpu.VMEM((2 * NROW, BLK, FS), F32),
            pltpu.VMEM((FS, FS), F32),
            pltpu.SemaphoreType.DMA((NCOL + 3,)),
        ],
        compiler_params=pltpu.CompilerParams(vmem_limit_bytes=LIMIT),
        cost_estimate=pl.CostEstimate(
            flops=6 * FRONT_ROWS * FRONT_COLS * FS, bytes_accessed=30 * 2**20, transcendentals=0
        ),
    )(table, ids, inverse, *row_pieces, *others, *arrived, *col_pieces)


def swap(value, axis, size, distance):
    if distance == 0:
        return value
    return lax.ppermute(value, axis, [(i, i ^ distance) for i in range(size)])


def tie(*values):
    return lax.optimization_barrier(values)


def body(child_upd, child_map, orig_pivot):
    ids = jnp.stack([lax.axis_index("sib"), lax.axis_index("row"), lax.axis_index("col")])
    ids = ids.astype(jnp.int32)
    x = child_upd[0]
    table = plan(child_map, ids)
    thin = pack_thin(child_map, ids, x)
    thin = lax.all_to_all(thin, "col", 0, 0, tiled=True)
    thin, part = place_thin(table, ids, thin)

    order = (1, 4, 6, 2, 5, 7, 3)
    first = list(pack_cols(child_map, ids, x, 0))
    first[1] = swap(first[1], "col", NCOL, 1)
    rounds = [("sib", 1), ("row", 4), ("row", 1), ("row", 2), None, None]
    for d, step in zip(order[1:], rounds):
        first[d] = swap(first[d], "col", NCOL, d)
        if step is not None:
            part = part + swap(part, step[0], 2 if step[0] == "sib" else 8, step[1])
        first[d], part = tie(first[d], part)

    packed, x, part = tie(pack_rows(0, table, thin, *first), x, part)
    arrived = lax.all_to_all(packed, ("sib", "row"), 0, 0, tiled=True)
    second = list(pack_cols(child_map, ids, x, 1))
    rounds = [4, 2, 1, None, None, None, None]
    for d, distance in zip(order, rounds):
        second[d] = swap(second[d], "col", NCOL, d)
        if distance is not None:
            part = jnp.concatenate([part, swap(part, "col", NCOL, distance)], 0)
        second[d], part = tie(second[d], part)

    arrived, second, part = tie(arrived, second, part)
    rows, cols = thin_rows(table, arrived)
    cols = jnp.concatenate([cols, swap(cols, "sib", 2, 1)], 0)
    rows = jnp.concatenate([rows, swap(rows, "row", NROW, 4)], 0)
    packed, cols, rows = tie(pack_rows(1, table, *first, *second), cols, rows)
    late = lax.all_to_all(packed, ("sib", "row"), 0, 0, tiled=True)
    c, r = {0: cols}, {0: rows}
    for d in (1, 3):
        c[2 * d], r[d] = swap(cols, "col", NCOL, 2 * d), swap(rows, "row", NROW, d)
    four = [VMEM] * 4
    factors = factor(factor_first_kernel, [SMEM, VMEM, VMEM], 10**10, ids, part, orig_pivot)
    factors = factor(functools.partial(factor_next_kernel, (1,)), four, 10**10, *factors)
    c, r, cols, rows, factors = tie(c, r, cols, rows, factors)
    c[4], r[2] = swap(cols, "col", NCOL, 4), swap(rows, "row", NROW, 2)
    for d in (0, 2, 6):
        c[d + 1] = swap(c[d], "col", NCOL, 1)
    factors = factor(functools.partial(factor_next_kernel, (2, 3)), four, 2 * 10**10, *factors)
    c, r, factors, late = tie(c, r, factors, late)
    c[5] = swap(c[4], "col", NCOL, 1)
    return update(
        table, ids, (arrived, late), factors, [c[d] for d in range(NCOL)], [r[d] for d in range(4)]
    )


def solution(mesh):
    return jax.shard_map(
        body,
        mesh=mesh,
        in_specs=(P("sib", "row", "col"), P(), P()),
        out_specs=P("row", ("sib", "col")),
        check_vma=False,
    )
```

```python
import functools

import jax
import jax.numpy as jnp
from jax import lax
from jax.experimental import pallas as pl
from jax.experimental.pallas import tpu as pltpu
from jax.sharding import PartitionSpec as P

BLK = 128
TILE = 256
NF = 20480
PANELS = 2
FS = PANELS * TILE
NROW = 8
NCOL = 8
PER = 8
FRONT_ROWS = NF // NROW
FRONT_COLS = NF // (2 * NCOL)
ROW_SLOTS = FRONT_ROWS // BLK
HALF_BLK = BLK // 2
THIN = 8 + 16 * PANELS
F32 = jnp.float32
VMEM = pl.BlockSpec(memory_space=pltpu.VMEM)
SMEM = pl.BlockSpec(memory_space=pltpu.SMEM)
ANY = pl.BlockSpec(memory_space=pl.ANY)
SPAN = 2 * TILE
LIMIT = 56 * 2**20


def product(left, right):
    return jnp.dot(left, right, precision=lax.Precision.HIGHEST, preferred_element_type=F32)


ROW_PLACE = 0
RANK = 8
HALF = 16
ROW_SLOT = 24
COL_SLOT = 40
PIVOT_ROW = 48
PIVOT_COL = 80
PLAN = 96


def split(value):
    high = value.astype(jnp.bfloat16)
    low = (value - high.astype(F32)).astype(jnp.bfloat16)
    return high, low


def product3(left, right):
    dot = lambda a, b: jnp.dot(a, b, preferred_element_type=F32)
    return dot(left[0], right[0]) + (dot(left[0], right[1]) + dot(left[1], right[0]))


def target(maps, child, line, place):
    return maps[child, 2 * ((place // 2) * NROW + line) + place % 2]


def class_of(block):
    return (block // 2) % NROW


def half_of(block):
    return (block // 2) // NROW % 2


def row_slot(block):
    return 2 * (block // 2 // NROW) + block % 2


def col_slot(block):
    return 2 * (block // 2 // (2 * NCOL)) + block % 2


def place_of(maps, child, line, wanted):
    found = jnp.int32(0)
    block = jnp.int32(0)
    for place in range(PER):
        here = target(maps, child, line, place)
        hit = class_of(here) == wanted
        found = jnp.where(hit, place, found)
        block = jnp.where(hit, here, block)
    return found, block


def at(index, size):
    return pl.ds(pl.multiple_of(index * size, size), size)


def plan_kernel(maps, ids, out):
    sib, row, col = ids[0], ids[1], ids[2]
    for dest in range(NROW):
        out[ROW_PLACE + dest] = place_of(maps, sib, row, dest)[0]
    blocks = [[place_of(maps, child, j, col)[1] for j in range(NCOL)] for child in range(2)]
    for d in range(NCOL):
        source = col ^ d
        block = place_of(maps, sib, source, col)[1]
        half = half_of(block)
        rank = jnp.int32(0)
        for j in range(NCOL):
            here = half_of(jnp.where(sib == 0, blocks[0][j], blocks[1][j])) == half
            rank += jnp.where((j < source) & here, 1, 0)
        out[RANK + d] = rank
        out[HALF + d] = half
        for b in range(PANELS):
            block = place_of(maps, sib, source, b)[1]
            out[PIVOT_COL + PANELS * d + b] = jnp.where(block // 2 == b, block, -1)
    for child in range(2):
        count = jnp.int32(0)
        found = [jnp.int32(0)] * 4
        for j in range(NCOL):
            block = blocks[child][j]
            mine = half_of(block) == sib
            for r in range(4):
                found[r] = jnp.where(mine & (count == r), col_slot(block), found[r])
            count += jnp.where(mine, 1, 0)
        for r in range(4):
            out[COL_SLOT + 4 * child + r] = found[r]
        for line in range(NROW):
            source = child * NROW + line
            out[ROW_SLOT + source] = row_slot(place_of(maps, child, line, row)[1])
            for a in range(PANELS):
                block = place_of(maps, child, line, a)[1]
                out[PIVOT_ROW + PANELS * source + a] = jnp.where(block // 2 == a, block, -1)


def plan(maps, ids):
    return pl.pallas_call(
        plan_kernel,
        out_shape=jax.ShapeDtypeStruct((PLAN,), jnp.int32),
        in_specs=[SMEM, SMEM],
        out_specs=SMEM,
        cost_estimate=pl.CostEstimate(flops=10**7, bytes_accessed=2**10, transcendentals=0),
    )(maps, ids)


def pack_thin_kernel(maps, ids, x_ref, out):
    child, col = ids[0], ids[2]
    for b in range(PANELS):
        q, _ = place_of(maps, child, col, b)
        for dest in range(NCOL):
            for p in range(PER):
                start = p * BLK + dest * 16
                out[dest, b, p * 16 : (p + 1) * 16, :] = x_ref[start : start + 16, at(q, BLK)]


def pack_thin(maps, ids, x):
    return pl.pallas_call(
        pack_thin_kernel,
        out_shape=jax.ShapeDtypeStruct((NCOL, PANELS, BLK, BLK), F32),
        in_specs=[SMEM, SMEM, VMEM],
        out_specs=VMEM,
        compiler_params=pltpu.CompilerParams(vmem_limit_bytes=LIMIT),
        cost_estimate=pl.CostEstimate(flops=0, bytes_accessed=6 * 2**20, transcendentals=0),
    )(maps, ids, x)


def place_thin_kernel(table, ids, in_ref, thin, pivot):
    child, row, col = ids[0], ids[1], ids[2]
    thin[...] = jnp.zeros_like(thin)
    pivot[...] = jnp.zeros_like(pivot)
    for d in range(NCOL):
        for b in range(PANELS):
            block = table[PIVOT_COL + PANELS * d + b]

            @pl.when(block >= 0)
            def _():
                thin[:, at(block, BLK)] = in_ref[col ^ d, b]

    for a in range(PANELS):
        block = table[PIVOT_ROW + PANELS * (child * NROW + row) + a]

        @pl.when(block >= 0)
        def _():
            pivot[at(block, 16), :] = thin[at(table[ROW_PLACE + a], 16), :]


def place_thin(table, ids, arrived):
    return pl.pallas_call(
        place_thin_kernel,
        out_shape=(jax.ShapeDtypeStruct((BLK, FS), F32), jax.ShapeDtypeStruct((FS // NCOL, FS), F32)),
        in_specs=[SMEM, SMEM, VMEM],
        out_specs=(VMEM, VMEM),
        compiler_params=pltpu.CompilerParams(vmem_limit_bytes=LIMIT),
        cost_estimate=pl.CostEstimate(flops=0, bytes_accessed=2 * 2**20, transcendentals=0),
    )(table, ids, arrived)


def pack_cols_kernel(classes, rows, maps, ids, x_ref, *out_refs):
    places = [place_of(maps, ids[0], ids[1], a)[0] for a in classes]
    for d in range(NCOL):
        lanes = at(place_of(maps, ids[0], ids[2], ids[2] ^ d)[0], BLK)
        for n, place in enumerate(places):
            out_refs[d // 2][d % 2, n] = x_ref[place, rows[0] : rows[1], lanes]


def pack_cols(maps, ids, x, classes, rows):
    shape = (2, len(classes), rows[1] - rows[0], BLK)
    return pl.pallas_call(
        functools.partial(pack_cols_kernel, classes, rows),
        out_shape=[jax.ShapeDtypeStruct(shape, F32)] * (NCOL // 2),
        in_specs=[SMEM, SMEM, VMEM],
        out_specs=[VMEM] * (NCOL // 2),
        compiler_params=pltpu.CompilerParams(vmem_limit_bytes=LIMIT),
        cost_estimate=pl.CostEstimate(flops=0, bytes_accessed=5 * 2**20, transcendentals=0),
    )(maps, ids, x.reshape(PER, BLK, PER * BLK))


def piece_of(chip_refs, core_refs, d):
    return core_refs[d // 2] if d % 2 else chip_refs[d // 2].at[0]


def pack_thin_rows_kernel(table, thin, *refs):
    out = refs[NCOL]
    for dest in range(NROW):
        place = table[ROW_PLACE + dest]
        for half in range(2):
            out[half * NROW + dest, :8, :] = thin[
                pl.ds(pl.multiple_of(place * 16 + half * 8, 8), 8), :
            ]
        for d in range(NCOL):
            half, lanes = table[HALF + d], at(table[RANK + d], BLK)
            piece = piece_of(refs[:4], refs[4:NCOL], d)
            for a in range(PANELS):
                out[half * NROW + dest, 8 + 16 * a : 24 + 16 * a, lanes] = piece[
                    a, dest * 16 : (dest + 1) * 16, :
                ]


def pack_thin_rows(table, thin, pieces):
    return pl.pallas_call(
        pack_thin_rows_kernel,
        out_shape=jax.ShapeDtypeStruct((2 * NROW, THIN, FS), F32),
        in_specs=[SMEM] + [VMEM] * (1 + NCOL),
        out_specs=VMEM,
        compiler_params=pltpu.CompilerParams(vmem_limit_bytes=LIMIT),
        cost_estimate=pl.CostEstimate(flops=0, bytes_accessed=4 * 2**20, transcendentals=0),
    )(table, thin, *pieces)


def pack_rows_kernel(part, table, *refs):
    first_refs, in_refs, out = refs[:NCOL], refs[NCOL : 2 * NCOL], refs[2 * NCOL]
    dest = pl.program_id(0)

    @pl.when(dest < PANELS)
    def _():
        for d in range(NCOL):
            piece = piece_of(first_refs[:4], first_refs[4:], d)
            out[table[HALF + d], 0, :, at(table[RANK + d], BLK)] = piece[
                jnp.minimum(dest, PANELS - 1), part * HALF_BLK : (part + 1) * HALF_BLK
            ]

    @pl.when(dest >= PANELS)
    def _():
        for d in range(NCOL):
            piece = piece_of(in_refs[:4], in_refs[4:], d)
            out[table[HALF + d], 0, :, at(table[RANK + d], BLK)] = piece[
                jnp.maximum(dest - PANELS, 0)
            ]


def pack_rows(table, part, first, others):
    return pl.pallas_call(
        functools.partial(pack_rows_kernel, part),
        grid=(NROW,),
        out_shape=jax.ShapeDtypeStruct((2, NROW, HALF_BLK, FS), F32),
        in_specs=[SMEM] + [VMEM] * (2 * NCOL),
        out_specs=pl.BlockSpec((2, 1, HALF_BLK, FS), lambda i: (0, i, 0, 0)),
        compiler_params=pltpu.CompilerParams(vmem_limit_bytes=LIMIT),
        cost_estimate=pl.CostEstimate(flops=0, bytes_accessed=6 * 2**20, transcendentals=0),
    )(table, *first, *others).reshape(2 * NROW, HALF_BLK, FS)


def thin_rows_kernel(table, in_ref, rows_ref, cols_ref):
    rows_ref[...] = jnp.zeros_like(rows_ref)
    for source in range(2 * NROW):
        cols_ref[source * 8 : (source + 1) * 8, :] = in_ref[source, :8, :]
        for a in range(PANELS):
            block = table[PIVOT_ROW + PANELS * source + a]

            @pl.when(block >= 0)
            def _():
                start = source // NROW * 64 + block * 16
                rows_ref[pl.ds(pl.multiple_of(start, 16), 16), :] = in_ref[
                    source, 8 + 16 * a : 24 + 16 * a, :
                ]


def thin_rows(table, arrived):
    out = jax.ShapeDtypeStruct((BLK, FS), F32)
    return pl.pallas_call(
        thin_rows_kernel,
        out_shape=(out, out),
        in_specs=[SMEM, VMEM],
        out_specs=(VMEM, VMEM),
        compiler_params=pltpu.CompilerParams(vmem_limit_bytes=LIMIT),
        cost_estimate=pl.CostEstimate(flops=0, bytes_accessed=2 * 2**20, transcendentals=0),
    )(table, arrived)


def invert_block(a, rows, cols):
    n = BLK
    lane8 = lax.broadcasted_iota(jnp.int32, (8, n), 1)
    row8 = lax.broadcasted_iota(jnp.int32, (8, n), 0)
    lane_rest = lax.broadcasted_iota(jnp.int32, (n - 8, n), 1)

    def across(x, j):
        return jnp.broadcast_to(x[:, j : j + 1], x.shape)

    def down(x, j):
        return jnp.broadcast_to(x[j : j + 1, :], x.shape)

    def group(g, s):
        top = s[:8]
        side = s[:, :8].T
        tops = [across(top, j) for j in range(8)]
        sides = [across(side, j) for j in range(8)]
        upper, lower = [], []
        for t in range(8):
            inv = 1.0 / down(tops[t], t)
            upper.append(top[t : t + 1, :])
            r = jnp.where(lane8 == t, 1.0, down(top, t)) * inv
            c = down(side, t)
            lower.append((c * inv)[0:1, :])
            rho = sides[t] * inv
            top = jnp.where(row8 == t, r, jnp.where(lane8 == t, 0.0, top) - tops[t] * r)
            side = jnp.where(lane8 == t, rho, side - rho * c)
            for j in range(t + 1, 8):
                scaled = down(tops[j], t) * inv
                tops[j] = jnp.where(row8 == t, scaled, tops[j] - tops[t] * scaled)
                sides[j] = sides[j] - down(sides[j], t) * rho
        rows[at(g, 8), :] = pltpu.roll(jnp.concatenate(upper, 0), g * 8, 1)
        cols[at(g, 8), :] = pltpu.roll(jnp.concatenate(lower, 0), g * 8, 1)
        rest = s[8:]
        new = jnp.where(lane_rest < 8, 0.0, rest)
        for j in range(8):
            new = new - across(rest, j) * jnp.broadcast_to(top[j : j + 1, :], rest.shape)
        return pltpu.roll(jnp.concatenate([new, top], 0), n - 8, 1)

    inverse = lax.fori_loop(0, n // 8, group, a)
    row = lax.broadcasted_iota(jnp.int32, (n, n), 0)
    lane = lax.broadcasted_iota(jnp.int32, (n, n), 1)
    eye = row == lane
    upper = rows[...]
    lower = cols[...].T
    packed = jnp.where(row > lane, lower, upper)
    lower_inv = jnp.where(row > lane, upper, jnp.where(eye, 1.0, 0.0))
    upper_inv = jnp.where(row < lane, -lower, jnp.where(eye, 1.0 / upper, 0.0))
    return inverse, packed, lower_inv, upper_inv


def eliminate(k, inv_ref, linv_ref, uinv_ref, lu_ref, rows, cols):
    count, n = FS // BLK, BLK
    lo, hi = k * n, (k + 1) * n
    inverse, packed, lower_inv, upper_inv = invert_block(inv_ref[lo:hi, lo:hi], rows, cols)
    x = inv_ref[lo:hi, :]
    y = inv_ref[:, lo:hi]
    scaled_rows = product(lower_inv, x)
    scaled_cols = product(y, upper_inv)
    lu_ref[lo:hi, lo:hi] = packed
    linv_ref[lo:hi, lo:hi] = lower_inv
    uinv_ref[lo:hi, lo:hi] = upper_inv
    if k > 0:
        linv_ref[lo:hi, :lo] = scaled_rows[:, :lo]
        uinv_ref[:lo, lo:hi] = -scaled_cols[:lo]
    if k < count - 1:
        lu_ref[lo:hi, hi:] = scaled_rows[:, hi:]
        lu_ref[hi:, lo:hi] = scaled_cols[hi:]
    inv_ref[lo:hi, :] = product(inverse, x)
    inv_ref[lo:hi, lo:hi] = inverse
    x = inv_ref[lo:hi, :]
    for i in range(count):
        if i != k:
            a, b = i * n, (i + 1) * n
            inv_ref[a:b, lo:hi] = jnp.zeros((n, n), F32)
            inv_ref[a:b, :] = inv_ref[a:b, :] - product(y[a:b], x)


def factor_first_kernel(ids, pieces_ref, orig_ref, inv_ref, linv_ref, uinv_ref, lu_ref, rows, cols):
    inv_ref[...] = orig_ref[...]
    for q in range(NCOL):
        owner = ids[2] ^ (4 * (q & 1) + (q & 2) + (q >> 2 & 1))
        for b in range(FS // BLK):
            start = q * (FS // NCOL) + b * 16
            place = pl.ds(pl.multiple_of(b * BLK + owner * 16, 16), 16)
            inv_ref[place, :] += pieces_ref[start : start + 16, :]
    linv_ref[...] = jnp.zeros_like(linv_ref)
    uinv_ref[...] = jnp.zeros_like(uinv_ref)
    lu_ref[...] = jnp.zeros_like(lu_ref)
    for k in range(2):
        eliminate(k, inv_ref, linv_ref, uinv_ref, lu_ref, rows, cols)


def factor_last_kernel(*refs):
    sources, dests, (rows, cols) = refs[:4], refs[4:8], refs[8:]
    for source, dest in zip(sources, dests):
        dest[...] = source[...]
    for k in range(2, FS // BLK):
        eliminate(k, *dests, rows, cols)


def factor(kernel, specs, *operands):
    square = jax.ShapeDtypeStruct((FS, FS), F32)
    return pl.pallas_call(
        kernel,
        out_shape=(square,) * 4,
        in_specs=specs,
        out_specs=(VMEM,) * 4,
        scratch_shapes=[pltpu.VMEM((BLK, BLK), F32)] * 2,
        compiler_params=pltpu.CompilerParams(vmem_limit_bytes=LIMIT),
        cost_estimate=pl.CostEstimate(
            flops=15 * 10**9, bytes_accessed=6 * 2**20, transcendentals=0
        ),
    )(*operands)


def update_kernel(table, ids, inv_ref, *refs):
    row_refs, linv_hbm, uinv_hbm, lu_hbm, arrived_hbm = refs[:4], *refs[4:7], refs[7:9]
    col_hbm, out_ref, scratch = refs[9 : 9 + NCOL], refs[9 + NCOL], refs[10 + NCOL :]
    left, left_parts, right_parts, pivots, cols, own, part, sems = scratch
    step = pl.program_id(0)
    sib, row, col = ids[0], ids[1], ids[2]
    group = sib * NCOL + col
    own_copies = [
        pltpu.make_async_copy(arrived_hbm[n], own.at[:, at(n, HALF_BLK)], sems.at[NCOL + n])
        for n in range(2)
    ]
    col_copies = [
        pltpu.make_async_copy(col_hbm[d], cols.at[d], sems.at[d]) for d in range(NCOL)
    ]
    part_sem = sems.at[NCOL + 2]

    @pl.when(step == 0)
    def _():
        for copy in col_copies + own_copies:
            copy.start()
        pivots[...] = jnp.zeros_like(pivots)
        for child in range(2):
            for r in range(4):
                lanes = at(table[COL_SLOT + 4 * child + r], BLK)
                for d in range(NROW):
                    for b in range(4):
                        start = (d // 4) * BLK + child * 64 + b * 16
                        rows = pl.ds(pl.multiple_of(b * BLK + (row ^ d) * 16, 16), 16)
                        pivots[rows, lanes] += row_refs[d % 4][
                            start : start + 16, r * BLK : (r + 1) * BLK
                        ]
        high, low = split(product3(split(-inv_ref[...]), split(pivots[...])))
        right_parts[:FS] = high
        right_parts[FS : 2 * FS] = low
        right_parts[2 * FS :] = high
        for copy in col_copies:
            copy.wait()

    left[...] = jnp.zeros_like(left)
    for source in range(2 * NROW):
        slot = table[ROW_SLOT + source]

        @pl.when(slot * BLK // SPAN == step)
        def _():
            for d in range(NCOL):
                for ds in range(2):
                    start = slot * BLK % SPAN + (col ^ d) * 16 + (sib ^ ds) * 8
                    left[pl.ds(pl.multiple_of(start, 8), 8), :] += cols[
                        d, ds * BLK + source * 8 : ds * BLK + source * 8 + 8, :
                    ]

    high, low = split(left[...])
    left_parts[:, :FS] = high
    left_parts[:, FS : 2 * FS] = high
    left_parts[:, 2 * FS :] = low
    out_ref[...] = jnp.dot(left_parts[...], right_parts[...], preferred_element_type=F32)

    @pl.when(step == 0)
    def _():
        for copy in own_copies:
            copy.wait()

    for source in range(2 * NROW):
        slot = table[ROW_SLOT + source]

        @pl.when(slot * BLK // SPAN == step)
        def _():
            rows = at(slot * BLK % SPAN // BLK, BLK)
            for r in range(4):
                lanes = at(table[COL_SLOT + source // NROW * 4 + r], BLK)
                out_ref[rows, lanes] += own[source, :, r * BLK : (r + 1) * BLK]

    @pl.when(group < PANELS)
    def _():
        copy = pltpu.make_async_copy(uinv_hbm, part, part_sem)
        copy.start()
        copy.wait()
        out_ref[:, :TILE] = product(left[...], part[:, at(group, TILE)])

    @pl.when((step == 0) & (row < PANELS))
    def _():
        copy = pltpu.make_async_copy(linv_hbm, part, part_sem)
        copy.start()
        copy.wait()
        out_ref[:TILE] = product(part[at(row, TILE), :], pivots[...])

        @pl.when(group < PANELS)
        def _():
            copy = pltpu.make_async_copy(lu_hbm, part, part_sem)
            copy.start()
            copy.wait()
            out_ref[:TILE, :TILE] = part[at(row, TILE), at(group, TILE)]


def update(table, ids, arrived, factors, col_pieces, row_pieces):
    inverse, *others = factors
    return pl.pallas_call(
        update_kernel,
        grid=(FRONT_ROWS // SPAN,),
        out_shape=jax.ShapeDtypeStruct((FRONT_ROWS, FRONT_COLS), F32),
        in_specs=[SMEM, SMEM] + [VMEM] * 5 + [ANY] * (5 + NCOL),
        out_specs=pl.BlockSpec((SPAN, FRONT_COLS), lambda i: (i, 0)),
        scratch_shapes=[
            pltpu.VMEM((SPAN, FS), F32),
            pltpu.VMEM((SPAN, 3 * FS), jnp.bfloat16),
            pltpu.VMEM((3 * FS, FRONT_COLS), jnp.bfloat16),
            pltpu.VMEM((FS, FRONT_COLS), F32),
            pltpu.VMEM((NCOL, 2 * BLK, FS), F32),
            pltpu.VMEM((2 * NROW, BLK, FS), F32),
            pltpu.VMEM((FS, FS), F32),
            pltpu.SemaphoreType.DMA((NCOL + 3,)),
        ],
        compiler_params=pltpu.CompilerParams(vmem_limit_bytes=LIMIT),
        cost_estimate=pl.CostEstimate(
            flops=6 * FRONT_ROWS * FRONT_COLS * FS, bytes_accessed=30 * 2**20, transcendentals=0
        ),
    )(table, ids, inverse, *row_pieces, *others, *arrived, *col_pieces)


def swap(value, axis, size, distance):
    if distance == 0:
        return value
    return lax.ppermute(value, axis, [(i, i ^ distance) for i in range(size)])


def tie(*values):
    return lax.optimization_barrier(values)


def body(child_upd, child_map, orig_pivot):
    ids = jnp.stack([lax.axis_index("sib"), lax.axis_index("row"), lax.axis_index("col")])
    ids = ids.astype(jnp.int32)
    x = child_upd[0]
    table = plan(child_map, ids)

    def over_chips(pieces):
        return [swap(piece, "col", NCOL, 2 * d) for d, piece in enumerate(pieces)]

    def over_cores(pieces):
        return list(pieces) + [swap(piece[1], "col", NCOL, 1) for piece in pieces]

    thin = pack_thin(child_map, ids, x)
    first = pack_cols(child_map, ids, x, range(PANELS), (0, BLK))
    thin, first, x = tie(thin, first, x)
    thin = lax.all_to_all(thin, "col", 0, 0, tiled=True)
    rest = range(PANELS, NROW)
    second = pack_cols(child_map, ids, x, rest, (0, HALF_BLK))
    third = list(pack_cols(child_map, ids, x, rest, (HALF_BLK, BLK)))

    first = over_chips(first)
    thin, part = place_thin(table, ids, thin)
    part = part + swap(part, "sib", 2, 1)
    part, first, second = tie(part, first, second)
    first = over_cores(first)
    part = part + swap(part, "row", 8, 4)

    packed = pack_thin_rows(table, thin, first)
    packed, second, part = tie(packed, second, part)
    early = lax.all_to_all(packed, ("sib", "row"), 0, 0, tiled=True)
    second = over_chips(second)
    part = part + swap(part, "row", 8, 1)
    early, second, third, part = tie(early, second, third, part)

    third[1], third[3] = swap(third[1], "col", NCOL, 2), swap(third[3], "col", NCOL, 6)
    rows, cols = thin_rows(table, early)
    cols = jnp.concatenate([cols, swap(cols, "sib", 2, 1)], 0)
    rows = jnp.concatenate([rows, swap(rows, "row", NROW, 4)], 0)
    part = part + swap(part, "row", 8, 2)
    packed = pack_rows(table, 0, first, over_cores(second))
    packed, cols, rows, part, third = tie(packed, cols, rows, part, third)
    arrived = lax.all_to_all(packed, ("sib", "row"), 0, 0, tiled=True)
    r = {0: rows, 1: swap(rows, "row", NROW, 1), 3: swap(rows, "row", NROW, 3)}
    third[2] = swap(third[2], "col", NCOL, 4)
    for distance in (4, 2):
        part = jnp.concatenate([part, swap(part, "col", NCOL, distance)], 0)

    packed = pack_rows(table, 1, first, over_cores(third))
    packed, part, cols, arrived = tie(packed, part, cols, arrived)
    late = lax.all_to_all(packed, ("sib", "row"), 0, 0, tiled=True)
    r[2] = swap(rows, "row", NROW, 2)
    part = jnp.concatenate([part, swap(part, "col", NCOL, 1)], 0)
    c = {2 * d: swap(cols, "col", NCOL, 2 * d) for d in (0, 1, 3, 2)}
    factors = factor(factor_first_kernel, [SMEM, VMEM, VMEM], ids, part, orig_pivot)
    c, factors = tie(c, factors)
    for d in (0, 2, 6, 4):
        c[d + 1] = swap(c[d], "col", NCOL, 1)
    factors = factor(factor_last_kernel, [VMEM] * 4, *factors)
    return update(
        table, ids, (arrived, late), factors, [c[d] for d in range(NCOL)], [r[d] for d in range(4)]
    )


def solution(mesh):
    return jax.shard_map(
        body,
        mesh=mesh,
        in_specs=(P("sib", "row", "col"), P(), P()),
        out_specs=P("row", ("sib", "col")),
        check_vma=False,
    )
```

```python
import functools

import jax
import jax.numpy as jnp
from jax import lax
from jax.experimental import pallas as pl
from jax.experimental.pallas import tpu as pltpu
from jax.sharding import PartitionSpec as P

BLK = 128
TILE = 256
NF = 20480
PANELS = 2
FS = PANELS * TILE
NROW = 8
NCOL = 8
PER = 8
FRONT_ROWS = NF // NROW
FRONT_COLS = NF // (2 * NCOL)
ROW_SLOTS = FRONT_ROWS // BLK
HALF_BLK = BLK // 2
THIN = 8 + 16 * PANELS
F32 = jnp.float32
VMEM = pl.BlockSpec(memory_space=pltpu.VMEM)
SMEM = pl.BlockSpec(memory_space=pltpu.SMEM)
ANY = pl.BlockSpec(memory_space=pl.ANY)
SPAN = 2 * TILE
LIMIT = 56 * 2**20


def product(left, right):
    return jnp.dot(left, right, precision=lax.Precision.HIGHEST, preferred_element_type=F32)


ROW_PLACE = 0
RANK = 8
HALF = 16
ROW_SLOT = 24
COL_SLOT = 40
PIVOT_ROW = 48
PIVOT_COL = 80
PLAN = 96


def split(value):
    high = value.astype(jnp.bfloat16)
    low = (value - high.astype(F32)).astype(jnp.bfloat16)
    return high, low


def product3(left, right):
    dot = lambda a, b: jnp.dot(a, b, preferred_element_type=F32)
    return dot(left[0], right[0]) + (dot(left[0], right[1]) + dot(left[1], right[0]))


def target(maps, child, line, place):
    return maps[child, 2 * ((place // 2) * NROW + line) + place % 2]


def class_of(block):
    return (block // 2) % NROW


def half_of(block):
    return (block // 2) // NROW % 2


def row_slot(block):
    return 2 * (block // 2 // NROW) + block % 2


def col_slot(block):
    return 2 * (block // 2 // (2 * NCOL)) + block % 2


def place_of(maps, child, line, wanted):
    found = jnp.int32(0)
    block = jnp.int32(0)
    for place in range(PER):
        here = target(maps, child, line, place)
        hit = class_of(here) == wanted
        found = jnp.where(hit, place, found)
        block = jnp.where(hit, here, block)
    return found, block


def at(index, size):
    return pl.ds(pl.multiple_of(index * size, size), size)


def plan_kernel(maps, ids, out):
    sib, row, col = ids[0], ids[1], ids[2]
    for dest in range(NROW):
        out[ROW_PLACE + dest] = place_of(maps, sib, row, dest)[0]
    blocks = [[place_of(maps, child, j, col)[1] for j in range(NCOL)] for child in range(2)]
    for d in range(NCOL):
        source = col ^ d
        block = place_of(maps, sib, source, col)[1]
        half = half_of(block)
        rank = jnp.int32(0)
        for j in range(NCOL):
            here = half_of(jnp.where(sib == 0, blocks[0][j], blocks[1][j])) == half
            rank += jnp.where((j < source) & here, 1, 0)
        out[RANK + d] = rank
        out[HALF + d] = half
        for b in range(PANELS):
            block = place_of(maps, sib, source, b)[1]
            out[PIVOT_COL + PANELS * d + b] = jnp.where(block // 2 == b, block, -1)
    for child in range(2):
        count = jnp.int32(0)
        found = [jnp.int32(0)] * 4
        for j in range(NCOL):
            block = blocks[child][j]
            mine = half_of(block) == sib
            for r in range(4):
                found[r] = jnp.where(mine & (count == r), col_slot(block), found[r])
            count += jnp.where(mine, 1, 0)
        for r in range(4):
            out[COL_SLOT + 4 * child + r] = found[r]
        for line in range(NROW):
            source = child * NROW + line
            out[ROW_SLOT + source] = row_slot(place_of(maps, child, line, row)[1])
            for a in range(PANELS):
                block = place_of(maps, child, line, a)[1]
                out[PIVOT_ROW + PANELS * source + a] = jnp.where(block // 2 == a, block, -1)


def plan(maps, ids):
    return pl.pallas_call(
        plan_kernel,
        out_shape=jax.ShapeDtypeStruct((PLAN,), jnp.int32),
        in_specs=[SMEM, SMEM],
        out_specs=SMEM,
        cost_estimate=pl.CostEstimate(flops=10**7, bytes_accessed=2**10, transcendentals=0),
    )(maps, ids)


def pack_thin_kernel(maps, ids, x_ref, out):
    child, col = ids[0], ids[2]
    for b in range(PANELS):
        q, _ = place_of(maps, child, col, b)
        for dest in range(NCOL):
            for p in range(PER):
                start = p * BLK + dest * 16
                out[dest, b, p * 16 : (p + 1) * 16, :] = x_ref[start : start + 16, at(q, BLK)]


def pack_thin(maps, ids, x):
    return pl.pallas_call(
        pack_thin_kernel,
        out_shape=jax.ShapeDtypeStruct((NCOL, PANELS, BLK, BLK), F32),
        in_specs=[SMEM, SMEM, VMEM],
        out_specs=VMEM,
        compiler_params=pltpu.CompilerParams(vmem_limit_bytes=LIMIT),
        cost_estimate=pl.CostEstimate(flops=0, bytes_accessed=6 * 2**20, transcendentals=0),
    )(maps, ids, x)


def place_thin_kernel(table, ids, in_ref, thin, pivot):
    child, row, col = ids[0], ids[1], ids[2]
    thin[...] = jnp.zeros_like(thin)
    pivot[...] = jnp.zeros_like(pivot)
    for d in range(NCOL):
        for b in range(PANELS):
            block = table[PIVOT_COL + PANELS * d + b]

            @pl.when(block >= 0)
            def _():
                thin[:, at(block, BLK)] = in_ref[col ^ d, b]

    for a in range(PANELS):
        block = table[PIVOT_ROW + PANELS * (child * NROW + row) + a]

        @pl.when(block >= 0)
        def _():
            pivot[at(block, 16), :] = thin[at(table[ROW_PLACE + a], 16), :]


def place_thin(table, ids, arrived):
    return pl.pallas_call(
        place_thin_kernel,
        out_shape=(jax.ShapeDtypeStruct((BLK, FS), F32), jax.ShapeDtypeStruct((FS // NCOL, FS), F32)),
        in_specs=[SMEM, SMEM, VMEM],
        out_specs=(VMEM, VMEM),
        compiler_params=pltpu.CompilerParams(vmem_limit_bytes=LIMIT),
        cost_estimate=pl.CostEstimate(flops=0, bytes_accessed=2 * 2**20, transcendentals=0),
    )(table, ids, arrived)


def pack_cols_kernel(classes, rows, maps, ids, x_ref, *out_refs):
    places = [place_of(maps, ids[0], ids[1], a)[0] for a in classes]
    for d in range(NCOL):
        lanes = at(place_of(maps, ids[0], ids[2], ids[2] ^ d)[0], BLK)
        for n, place in enumerate(places):
            out_refs[d // 2][d % 2, n] = x_ref[place, rows[0] : rows[1], lanes]


def pack_cols(maps, ids, x, classes, rows):
    shape = (2, len(classes), rows[1] - rows[0], BLK)
    return pl.pallas_call(
        functools.partial(pack_cols_kernel, classes, rows),
        out_shape=[jax.ShapeDtypeStruct(shape, F32)] * (NCOL // 2),
        in_specs=[SMEM, SMEM, VMEM],
        out_specs=[VMEM] * (NCOL // 2),
        compiler_params=pltpu.CompilerParams(vmem_limit_bytes=LIMIT),
        cost_estimate=pl.CostEstimate(flops=0, bytes_accessed=5 * 2**20, transcendentals=0),
    )(maps, ids, x.reshape(PER, BLK, PER * BLK))


def piece_of(chip_refs, core_refs, d):
    return core_refs[d // 2] if d % 2 else chip_refs[d // 2].at[0]


def pack_thin_rows_kernel(table, thin, *refs):
    out = refs[NCOL]
    for dest in range(NROW):
        place = table[ROW_PLACE + dest]
        for half in range(2):
            out[half * NROW + dest, :8, :] = thin[
                pl.ds(pl.multiple_of(place * 16 + half * 8, 8), 8), :
            ]
        for d in range(NCOL):
            half, lanes = table[HALF + d], at(table[RANK + d], BLK)
            piece = piece_of(refs[:4], refs[4:NCOL], d)
            for a in range(PANELS):
                out[half * NROW + dest, 8 + 16 * a : 24 + 16 * a, lanes] = piece[
                    a, dest * 16 : (dest + 1) * 16, :
                ]


def pack_thin_rows(table, thin, pieces):
    return pl.pallas_call(
        pack_thin_rows_kernel,
        out_shape=jax.ShapeDtypeStruct((2 * NROW, THIN, FS), F32),
        in_specs=[SMEM] + [VMEM] * (1 + NCOL),
        out_specs=VMEM,
        compiler_params=pltpu.CompilerParams(vmem_limit_bytes=LIMIT),
        cost_estimate=pl.CostEstimate(flops=0, bytes_accessed=4 * 2**20, transcendentals=0),
    )(table, thin, *pieces)


def pack_rows_kernel(part, table, *refs):
    first_refs, in_refs, out = refs[:NCOL], refs[NCOL : 2 * NCOL], refs[2 * NCOL]
    dest = pl.program_id(0)

    @pl.when(dest < PANELS)
    def _():
        for d in range(NCOL):
            piece = piece_of(first_refs[:4], first_refs[4:], d)
            out[table[HALF + d], 0, :, at(table[RANK + d], BLK)] = piece[
                jnp.minimum(dest, PANELS - 1), part * HALF_BLK : (part + 1) * HALF_BLK
            ]

    @pl.when(dest >= PANELS)
    def _():
        for d in range(NCOL):
            piece = piece_of(in_refs[:4], in_refs[4:], d)
            out[table[HALF + d], 0, :, at(table[RANK + d], BLK)] = piece[
                jnp.maximum(dest - PANELS, 0)
            ]


def pack_rows(table, part, first, others):
    return pl.pallas_call(
        functools.partial(pack_rows_kernel, part),
        grid=(NROW,),
        out_shape=jax.ShapeDtypeStruct((2, NROW, HALF_BLK, FS), F32),
        in_specs=[SMEM] + [VMEM] * (2 * NCOL),
        out_specs=pl.BlockSpec((2, 1, HALF_BLK, FS), lambda i: (0, i, 0, 0)),
        compiler_params=pltpu.CompilerParams(vmem_limit_bytes=LIMIT),
        cost_estimate=pl.CostEstimate(flops=0, bytes_accessed=6 * 2**20, transcendentals=0),
    )(table, *first, *others).reshape(2 * NROW, HALF_BLK, FS)


def thin_rows_kernel(table, in_ref, rows_ref, cols_ref):
    rows_ref[...] = jnp.zeros_like(rows_ref)
    for source in range(2 * NROW):
        cols_ref[source * 8 : (source + 1) * 8, :] = in_ref[source, :8, :]
        for a in range(PANELS):
            block = table[PIVOT_ROW + PANELS * source + a]

            @pl.when(block >= 0)
            def _():
                start = source // NROW * 64 + block * 16
                rows_ref[pl.ds(pl.multiple_of(start, 16), 16), :] = in_ref[
                    source, 8 + 16 * a : 24 + 16 * a, :
                ]


def thin_rows(table, arrived):
    out = jax.ShapeDtypeStruct((BLK, FS), F32)
    return pl.pallas_call(
        thin_rows_kernel,
        out_shape=(out, out),
        in_specs=[SMEM, VMEM],
        out_specs=(VMEM, VMEM),
        compiler_params=pltpu.CompilerParams(vmem_limit_bytes=LIMIT),
        cost_estimate=pl.CostEstimate(flops=0, bytes_accessed=2 * 2**20, transcendentals=0),
    )(table, arrived)


def invert_block(a, rows, cols):
    n = BLK
    lane8 = lax.broadcasted_iota(jnp.int32, (8, n), 1)
    row8 = lax.broadcasted_iota(jnp.int32, (8, n), 0)
    lane_rest = lax.broadcasted_iota(jnp.int32, (n - 8, n), 1)

    def across(x, j):
        return jnp.broadcast_to(x[:, j : j + 1], x.shape)

    def down(x, j):
        return jnp.broadcast_to(x[j : j + 1, :], x.shape)

    def group(g, s):
        top = s[:8]
        side = s[:, :8].T
        tops = [across(top, j) for j in range(8)]
        sides = [across(side, j) for j in range(8)]
        upper, lower = [], []
        for t in range(8):
            inv = 1.0 / down(tops[t], t)
            upper.append(top[t : t + 1, :])
            r = jnp.where(lane8 == t, 1.0, down(top, t)) * inv
            c = down(side, t)
            lower.append((c * inv)[0:1, :])
            rho = sides[t] * inv
            top = jnp.where(row8 == t, r, jnp.where(lane8 == t, 0.0, top) - tops[t] * r)
            side = jnp.where(lane8 == t, rho, side - rho * c)
            for j in range(t + 1, 8):
                scaled = down(tops[j], t) * inv
                tops[j] = jnp.where(row8 == t, scaled, tops[j] - tops[t] * scaled)
                sides[j] = sides[j] - down(sides[j], t) * rho
        rows[at(g, 8), :] = pltpu.roll(jnp.concatenate(upper, 0), g * 8, 1)
        cols[at(g, 8), :] = pltpu.roll(jnp.concatenate(lower, 0), g * 8, 1)
        rest = s[8:]
        new = jnp.where(lane_rest < 8, 0.0, rest)
        for j in range(8):
            new = new - across(rest, j) * jnp.broadcast_to(top[j : j + 1, :], rest.shape)
        return pltpu.roll(jnp.concatenate([new, top], 0), n - 8, 1)

    inverse = lax.fori_loop(0, n // 8, group, a)
    row = lax.broadcasted_iota(jnp.int32, (n, n), 0)
    lane = lax.broadcasted_iota(jnp.int32, (n, n), 1)
    eye = row == lane
    upper = rows[...]
    lower = cols[...].T
    packed = jnp.where(row > lane, lower, upper)
    lower_inv = jnp.where(row > lane, upper, jnp.where(eye, 1.0, 0.0))
    upper_inv = jnp.where(row < lane, -lower, jnp.where(eye, 1.0 / upper, 0.0))
    return inverse, packed, lower_inv, upper_inv


def eliminate(k, inv_ref, linv_ref, uinv_ref, lu_ref, rows, cols):
    count, n = FS // BLK, BLK
    lo, hi = k * n, (k + 1) * n
    inverse, packed, lower_inv, upper_inv = invert_block(inv_ref[lo:hi, lo:hi], rows, cols)
    x = inv_ref[lo:hi, :]
    y = inv_ref[:, lo:hi]
    scaled_rows = product(lower_inv, x)
    scaled_cols = product(y, upper_inv)
    lu_ref[lo:hi, lo:hi] = packed
    linv_ref[lo:hi, lo:hi] = lower_inv
    uinv_ref[lo:hi, lo:hi] = upper_inv
    if k > 0:
        linv_ref[lo:hi, :lo] = scaled_rows[:, :lo]
        uinv_ref[:lo, lo:hi] = -scaled_cols[:lo]
    if k < count - 1:
        lu_ref[lo:hi, hi:] = scaled_rows[:, hi:]
        lu_ref[hi:, lo:hi] = scaled_cols[hi:]
    inv_ref[lo:hi, :] = product(inverse, x)
    inv_ref[lo:hi, lo:hi] = inverse
    x = inv_ref[lo:hi, :]
    for i in range(count):
        if i != k:
            a, b = i * n, (i + 1) * n
            inv_ref[a:b, lo:hi] = jnp.zeros((n, n), F32)
            inv_ref[a:b, :] = inv_ref[a:b, :] - product(y[a:b], x)


def factor_first_kernel(ids, pieces_ref, orig_ref, inv_ref, linv_ref, uinv_ref, lu_ref, rows, cols):
    inv_ref[...] = orig_ref[...]
    for q in range(NCOL):
        owner = ids[2] ^ (4 * (q & 1) + (q & 2) + (q >> 2 & 1))
        for b in range(FS // BLK):
            start = q * (FS // NCOL) + b * 16
            place = pl.ds(pl.multiple_of(b * BLK + owner * 16, 16), 16)
            inv_ref[place, :] += pieces_ref[start : start + 16, :]
    linv_ref[...] = jnp.zeros_like(linv_ref)
    uinv_ref[...] = jnp.zeros_like(uinv_ref)
    lu_ref[...] = jnp.zeros_like(lu_ref)
    for k in range(2):
        eliminate(k, inv_ref, linv_ref, uinv_ref, lu_ref, rows, cols)


def factor_last_kernel(*refs):
    sources, dests, (rows, cols) = refs[:4], refs[4:8], refs[8:]
    for source, dest in zip(sources, dests):
        dest[...] = source[...]
    for k in range(2, FS // BLK):
        eliminate(k, *dests, rows, cols)


def factor(kernel, specs, *operands):
    square = jax.ShapeDtypeStruct((FS, FS), F32)
    return pl.pallas_call(
        kernel,
        out_shape=(square,) * 4,
        in_specs=specs,
        out_specs=(VMEM,) * 4,
        scratch_shapes=[pltpu.VMEM((BLK, BLK), F32)] * 2,
        compiler_params=pltpu.CompilerParams(vmem_limit_bytes=LIMIT),
        cost_estimate=pl.CostEstimate(
            flops=15 * 10**9, bytes_accessed=6 * 2**20, transcendentals=0
        ),
    )(*operands)


def update_kernel(table, ids, inv_ref, *refs):
    row_refs, linv_hbm, uinv_hbm, lu_hbm, arrived_hbm = refs[:4], *refs[4:7], refs[7:9]
    col_hbm, out_ref, scratch = refs[9 : 9 + NCOL], refs[9 + NCOL], refs[10 + NCOL :]
    left, left_parts, right_parts, pivots, cols, own, others, solve, sems = scratch
    step = pl.program_id(0)
    sib, row, col = ids[0], ids[1], ids[2]
    group = sib * NCOL + col
    own_copies = [
        pltpu.make_async_copy(arrived_hbm[n], own.at[:, at(n, HALF_BLK)], sems.at[NCOL + n])
        for n in range(2)
    ]
    col_copies = [
        pltpu.make_async_copy(col_hbm[d], cols.at[d], sems.at[d]) for d in range(NCOL)
    ]
    other_copies = [
        pltpu.make_async_copy(ref, others.at[n], sems.at[NCOL + 2 + n])
        for n, ref in enumerate((uinv_hbm, linv_hbm, lu_hbm))
    ]

    @pl.when(step == 0)
    def _():
        for copy in col_copies + own_copies + other_copies:
            copy.start()
        pivots[...] = jnp.zeros_like(pivots)
        for child in range(2):
            for r in range(4):
                lanes = at(table[COL_SLOT + 4 * child + r], BLK)
                for d in range(NROW):
                    for b in range(4):
                        start = (d // 4) * BLK + child * 64 + b * 16
                        rows = pl.ds(pl.multiple_of(b * BLK + (row ^ d) * 16, 16), 16)
                        pivots[rows, lanes] += row_refs[d % 4][
                            start : start + 16, r * BLK : (r + 1) * BLK
                        ]
        high, low = split(product3(split(-inv_ref[...]), split(pivots[...])))
        right_parts[:FS] = high
        right_parts[FS : 2 * FS] = low
        right_parts[2 * FS :] = high
        for copy in col_copies + other_copies:
            copy.wait()

        @pl.when(group < PANELS)
        def _():
            high, low = split(others[0, :, at(group, TILE)])
            solve[:FS] = high
            solve[FS : 2 * FS] = low
            solve[2 * FS :] = high

    left[...] = jnp.zeros_like(left)
    for source in range(2 * NROW):
        slot = table[ROW_SLOT + source]

        @pl.when(slot * BLK // SPAN == step)
        def _():
            for d in range(NCOL):
                for ds in range(2):
                    start = slot * BLK % SPAN + (col ^ d) * 16 + (sib ^ ds) * 8
                    left[pl.ds(pl.multiple_of(start, 8), 8), :] += cols[
                        d, ds * BLK + source * 8 : ds * BLK + source * 8 + 8, :
                    ]

    high, low = split(left[...])
    left_parts[:, :FS] = high
    left_parts[:, FS : 2 * FS] = high
    left_parts[:, 2 * FS :] = low
    out_ref[...] = jnp.dot(left_parts[...], right_parts[...], preferred_element_type=F32)

    @pl.when(step == 0)
    def _():
        for copy in own_copies:
            copy.wait()

    for source in range(2 * NROW):
        slot = table[ROW_SLOT + source]

        @pl.when(slot * BLK // SPAN == step)
        def _():
            rows = at(slot * BLK % SPAN // BLK, BLK)
            for r in range(4):
                lanes = at(table[COL_SLOT + source // NROW * 4 + r], BLK)
                out_ref[rows, lanes] += own[source, :, r * BLK : (r + 1) * BLK]

    @pl.when(group < PANELS)
    def _():
        out_ref[:, :TILE] = jnp.dot(left_parts[...], solve[...], preferred_element_type=F32)

    @pl.when((step == 0) & (row < PANELS))
    def _():
        out_ref[:TILE] = product3(split(others[1, at(row, TILE), :]), split(pivots[...]))

        @pl.when(group < PANELS)
        def _():
            out_ref[:TILE, :TILE] = others[2, at(row, TILE), at(group, TILE)]


def update(table, ids, arrived, factors, col_pieces, row_pieces):
    inverse, *others = factors
    return pl.pallas_call(
        update_kernel,
        grid=(FRONT_ROWS // SPAN,),
        out_shape=jax.ShapeDtypeStruct((FRONT_ROWS, FRONT_COLS), F32),
        in_specs=[SMEM, SMEM] + [VMEM] * 5 + [ANY] * (5 + NCOL),
        out_specs=pl.BlockSpec((SPAN, FRONT_COLS), lambda i: (i, 0)),
        scratch_shapes=[
            pltpu.VMEM((SPAN, FS), F32),
            pltpu.VMEM((SPAN, 3 * FS), jnp.bfloat16),
            pltpu.VMEM((3 * FS, FRONT_COLS), jnp.bfloat16),
            pltpu.VMEM((FS, FRONT_COLS), F32),
            pltpu.VMEM((NCOL, 2 * BLK, FS), F32),
            pltpu.VMEM((2 * NROW, BLK, FS), F32),
            pltpu.VMEM((3, FS, FS), F32),
            pltpu.VMEM((3 * FS, TILE), jnp.bfloat16),
            pltpu.SemaphoreType.DMA((NCOL + 5,)),
        ],
        compiler_params=pltpu.CompilerParams(vmem_limit_bytes=LIMIT),
        cost_estimate=pl.CostEstimate(
            flops=6 * FRONT_ROWS * FRONT_COLS * FS, bytes_accessed=30 * 2**20, transcendentals=0
        ),
    )(table, ids, inverse, *row_pieces, *others, *arrived, *col_pieces)


def swap(value, axis, size, distance):
    if distance == 0:
        return value
    return lax.ppermute(value, axis, [(i, i ^ distance) for i in range(size)])


def tie(*values):
    return lax.optimization_barrier(values)


def body(child_upd, child_map, orig_pivot):
    ids = jnp.stack([lax.axis_index("sib"), lax.axis_index("row"), lax.axis_index("col")])
    ids = ids.astype(jnp.int32)
    x = child_upd[0]
    table = plan(child_map, ids)

    def over_chips(pieces):
        return [swap(piece, "col", NCOL, 2 * d) for d, piece in enumerate(pieces)]

    def over_cores(pieces):
        return list(pieces) + [swap(piece[1], "col", NCOL, 1) for piece in pieces]

    thin = pack_thin(child_map, ids, x)
    first = pack_cols(child_map, ids, x, range(PANELS), (0, BLK))
    thin, first, x = tie(thin, first, x)
    thin = lax.all_to_all(thin, "col", 0, 0, tiled=True)
    rest = range(PANELS, NROW)
    second = pack_cols(child_map, ids, x, rest, (0, HALF_BLK))
    third = list(pack_cols(child_map, ids, x, rest, (HALF_BLK, BLK)))

    first = over_chips(first)
    thin, part = place_thin(table, ids, thin)
    part = part + swap(part, "sib", 2, 1)
    part, first, second = tie(part, first, second)
    first = over_cores(first)
    part = part + swap(part, "row", 8, 4)

    packed = pack_thin_rows(table, thin, first)
    packed, second, part = tie(packed, second, part)
    early = lax.all_to_all(packed, ("sib", "row"), 0, 0, tiled=True)
    second = over_chips(second)
    part = part + swap(part, "row", 8, 1)
    early, second, third, part = tie(early, second, third, part)

    third[1], third[3] = swap(third[1], "col", NCOL, 2), swap(third[3], "col", NCOL, 6)
    rows, cols = thin_rows(table, early)
    cols = jnp.concatenate([cols, swap(cols, "sib", 2, 1)], 0)
    rows = jnp.concatenate([rows, swap(rows, "row", NROW, 4)], 0)
    part = part + swap(part, "row", 8, 2)
    packed = pack_rows(table, 0, first, over_cores(second))
    packed, cols, rows, part, third = tie(packed, cols, rows, part, third)
    arrived = lax.all_to_all(packed, ("sib", "row"), 0, 0, tiled=True)
    r = {0: rows, 1: swap(rows, "row", NROW, 1), 3: swap(rows, "row", NROW, 3)}
    third[2] = swap(third[2], "col", NCOL, 4)
    for distance in (4, 2):
        part = jnp.concatenate([part, swap(part, "col", NCOL, distance)], 0)

    packed = pack_rows(table, 1, first, over_cores(third))
    packed, part, cols, arrived = tie(packed, part, cols, arrived)
    late = lax.all_to_all(packed, ("sib", "row"), 0, 0, tiled=True)
    r[2] = swap(rows, "row", NROW, 2)
    part = jnp.concatenate([part, swap(part, "col", NCOL, 1)], 0)
    c = {2 * d: swap(cols, "col", NCOL, 2 * d) for d in (0, 1, 3, 2)}
    factors = factor(factor_first_kernel, [SMEM, VMEM, VMEM], ids, part, orig_pivot)
    c, factors = tie(c, factors)
    for d in (0, 2, 6, 4):
        c[d + 1] = swap(c[d], "col", NCOL, 1)
    factors = factor(factor_last_kernel, [VMEM] * 4, *factors)
    return update(
        table, ids, (arrived, late), factors, [c[d] for d in range(NCOL)], [r[d] for d in range(4)]
    )


def solution(mesh):
    return jax.shard_map(
        body,
        mesh=mesh,
        in_specs=(P("sib", "row", "col"), P(), P()),
        out_specs=P("row", ("sib", "col")),
        check_vma=False,
    )
```
